128 devices in a mesh: ctx: 8 (over y_lo, z), head: 16 (over y_hi, x, core).
Axes of the slice: x: 4, y: 4 (y_hi: 2, y_lo: 2; y = y_hi * 2 + y_lo), z: 4, core: 2. Of those that a mesh axis runs over, the one named last changes fastest.
Arguments:
- queries: bfloat16 [4096, 8192], P('ctx', 'head'), may hold values from -108 to 108
- key_heads: bfloat16 [4096, 1024], P('ctx'), may hold values from -4.5 to 4.5
- values: bfloat16 [4096, 1024], P('ctx'), may hold values from -6 to 6
- log_decay: float32 [4096, 64], P('ctx', 'head'), may hold values from -1 to 0, as said below
- write_strength: float32 [4096, 64], P('ctx', 'head'), may hold values from 0.1 to 0.9
- query_map: bfloat16 [64, 128, 128], P('head'), may hold values from -0.5 to 0.5
- key_map: bfloat16 [64, 128, 128], P('head'), may hold values from -0.5 to 0.5
- out_weight: bfloat16 [8192, 8192], P('head'), may hold values from -0.09375 to 0.09375
Outputs:
- mean_square: float32 [], replicated
- query_map_grad: float32 [64, 128, 128], P('head')
- key_map_grad: float32 [64, 128, 128], P('head')
The draws below stay inside these ranges and needn't reach their ends.
Inputs may be any that keep to these rules, and one draw needn't show every extreme that they name: `log_decay`: log decays are negative.
All inputs are finite; a program needn't handle non-finite values.
Results may differ from the reference program's by a relative error of at most 0.0024.
Values may be sent and summed in bfloat16 or wider, within the bound.
No kernel may reach another device: no remote copies, remote signals or barrier semaphores. Data moves between devices by JAX's collectives and lax.ppermute only.
A program may use at most 192 MiB of HBM per device.

```python
import math
import jax
import jax.numpy as jnp
from jax import lax

D = 8192
QUERY_HEAD_COUNT = 64
KVH = 8
HD = 128
SPAN = 64
TOK_DEV = 512
TOKEN_COUNT = 4096


def shared_keys(key):
    normal_draw = jax.random.normal(jax.random.fold_in(key, 17), (TOKEN_COUNT, KVH * HD), jnp.float32)
    return jnp.clip(normal_draw, -4.5, 4.5)


def draw_key_heads(key, part):
    base_keys = shared_keys(key)
    return base_keys.astype(jnp.bfloat16)


def draw_queries(key, part):
    key = jax.random.fold_in(key, 2)
    query_draw = jnp.clip(jax.random.normal(key, (TOKEN_COUNT, QUERY_HEAD_COUNT * HD), jnp.float32), -4.5, 4.5)
    return query_draw.astype(jnp.bfloat16)


def draw_log_decay(key, part):
    key = jax.random.fold_in(key, 3)
    random_child_keys = jax.random.split(key, 7)
    fast_share = 0.5
    fast_heads = jax.random.bernoulli(random_child_keys[0], fast_share, (QUERY_HEAD_COUNT,))
    fast_rate = jnp.exp(jax.random.uniform(random_child_keys[1], (QUERY_HEAD_COUNT,), jnp.float32, jnp.log(1.0 / 50.0), jnp.log(1.0 / 30.0)))
    slow_rate = jnp.exp(jax.random.uniform(random_child_keys[2], (QUERY_HEAD_COUNT,), jnp.float32, jnp.log(0.05), jnp.log(0.5))) / TOKEN_COUNT
    decay_rate = jnp.where(fast_heads, fast_rate, slow_rate)
    block_total = TOKEN_COUNT // TOK_DEV
    scale_per_block = jnp.exp(jax.random.uniform(random_child_keys[3], (block_total, 1, QUERY_HEAD_COUNT), jnp.float32, jnp.log(0.5), jnp.log(2.0)))
    roughness = jax.random.uniform(random_child_keys[4], (block_total, TOK_DEV, QUERY_HEAD_COUNT), jnp.float32, 0.5, 1.5)
    logarithmic_rate = -(decay_rate * scale_per_block * roughness).reshape(TOKEN_COUNT, QUERY_HEAD_COUNT)
    segment_rows = jax.random.randint(random_child_keys[5], (2,), 0, TOKEN_COUNT)
    segment_length = jax.random.uniform(random_child_keys[6], (2, QUERY_HEAD_COUNT), jnp.float32, 0.22, 0.69)
    return logarithmic_rate.at[segment_rows].add(-segment_length)


def raised(drawn, stream_key, source, target, shards_of, factor):
    def block_of(axis_at):
        return (jnp.arange(drawn.shape[axis_at]) // (drawn.shape[axis_at] // shards_of)).reshape((-1,) + (1,) * (drawn.ndim - 1 - axis_at))

    first = jax.random.permutation(stream_key, shards_of)[block_of(target)]
    far = (block_of(target) + shards_of // 2) % shards_of
    return jnp.where((block_of(source) == first) | (block_of(source) == far), factor * drawn, drawn)


def levels(rng, dims, cuts, smallest, high):
    factor_of = 1.0
    for dim, shards_of in cuts:
        draws = jax.random.uniform(jax.random.fold_in(jax.random.fold_in(rng, 6), dim), (shards_of,), jnp.float32, smallest / len(cuts), high / len(cuts))
        factor_of = factor_of * jnp.repeat(jnp.exp(draws), dims[dim] // shards_of).reshape((-1,) + (1,) * (len(dims) - 1 - dim))
    return factor_of


def scatter_about(key, shape, deviation, most, shards=(), kind=jnp.bfloat16):
    values = deviation * jax.random.normal(key, shape, jnp.float32)
    if shards:
        values = values * levels(key, shape, shards, -0.22, 0.18)
    return jnp.clip(values, -most, most).astype(kind)


def noise_with(own_key, dims, spread, limit, cuts, heavy, held_as=jnp.bfloat16):
    values = spread * jax.random.normal(own_key, dims, jnp.float32)
    if cuts:
        values = values * levels(own_key, dims, cuts, -0.22, 0.18)
    return jnp.clip(raised(values, jax.random.fold_in(own_key, 3), *heavy), -limit, limit).astype(held_as)


def setup_inputs(seed: int = 0) -> dict:
    streams_of = jax.random.split(jax.random.key(seed), 9)
    return {
        "queries": draw_queries(jax.random.fold_in(streams_of[8], 71), 0),
        "key_heads": draw_key_heads(jax.random.fold_in(streams_of[8], 71), 0),
        "values": scatter_about(streams_of[2], (TOKEN_COUNT, KVH * HD), 1.0, 6.0, ((0, 8),)),
        "log_decay": draw_log_decay(jax.random.fold_in(streams_of[8], 71), 0),
        "write_strength": jnp.clip(0.1 + 0.79999997 * jax.random.uniform(streams_of[4], (TOKEN_COUNT, QUERY_HEAD_COUNT), jnp.float32) ** levels(streams_of[4], (TOKEN_COUNT, QUERY_HEAD_COUNT), ((0, 8), (1, 16)), -0.2, 0.2), 0.1, 0.9),
        "query_map": scatter_about(streams_of[5], (QUERY_HEAD_COUNT, HD, HD), HD ** -0.5, 0.5, ((0, 16),)),
        "key_map": scatter_about(streams_of[6], (QUERY_HEAD_COUNT, HD, HD), HD ** -0.5, 0.5, ((0, 16),)),
        "out_weight": noise_with(streams_of[7], (QUERY_HEAD_COUNT * HD, D), (QUERY_HEAD_COUNT * HD) ** -0.5, 0.09375, ((0, 16),), (0, 1, 16, 2.0)),
    }


BEST_PRECISION = lax.Precision.HIGHEST

def unit_rows(vector):
    return vector / jnp.sqrt(lax.optimization_barrier(jnp.sum(vector * vector, axis=-1, keepdims=True)) + 1e-06)

def span_step(state, inputs):
    query_block, key_block, value_block, gate_block, write_block = inputs
    block_len = query_block.shape[1]
    state_width = state.shape[2]
    cumulative = jnp.cumsum(gate_block, axis=1)
    position = jnp.arange(block_len)
    strict = position[:, None] > position[None, :]
    inclusive = position[:, None] >= position[None, :]
    log_gap = cumulative[:, :, None] - cumulative[:, None, :]
    decay_strict = jnp.where(strict, jnp.exp(jnp.where(strict, log_gap, 0.0)), 0.0)
    decay_inclusive = jnp.where(inclusive, jnp.exp(jnp.where(inclusive, log_gap, 0.0)), 0.0)
    key_gram = jnp.einsum('hid,hjd->hij', key_block, key_block, precision=BEST_PRECISION)
    system = write_block[:, :, None] * decay_strict * key_gram + jnp.eye(block_len, dtype=key_block.dtype)
    growth = jnp.exp(cumulative)
    right_side = jnp.concatenate([write_block[:, :, None] * value_block, (write_block * growth)[:, :, None] * key_block], axis=2)
    solved = jax.scipy.linalg.solve_triangular(system, right_side, lower=True, unit_diagonal=True)
    updates = solved[:, :, :state_width] - jnp.einsum('hcd,hdw->hcw', solved[:, :, state_width:], state, precision=BEST_PRECISION)
    query_key = jnp.einsum('hid,hjd->hij', query_block, key_block, precision=BEST_PRECISION)
    outputs = growth[:, :, None] * jnp.einsum('hcd,hdw->hcw', query_block, state, precision=BEST_PRECISION)
    outputs = outputs + jnp.einsum('hij,hjw->hiw', decay_inclusive * query_key, updates, precision=BEST_PRECISION)
    tail_decay = jnp.exp(cumulative[:, -1:] - cumulative)
    new_state = growth[:, -1][:, None, None] * state + jnp.einsum('hcd,hcw->hdw', key_block * tail_decay[:, :, None], updates, precision=BEST_PRECISION)
    return (new_state, outputs)

def run_spans(state, unit_query, unit_key, value_rows, gates, writes, block_len):
    head_count = unit_query.shape[0]
    length = unit_query.shape[1]
    block_count = length // block_len

    def to_blocks(tensor):
        return jnp.moveaxis(tensor.reshape((head_count, block_count, block_len) + tensor.shape[2:]), 1, 0)
    last_state, outputs = lax.scan(span_step, state, (to_blocks(unit_query), to_blocks(unit_key), to_blocks(value_rows), to_blocks(gates), to_blocks(writes)))
    outputs = jnp.moveaxis(outputs, 0, 1).reshape(head_count, length, outputs.shape[-1])
    return (last_state, outputs)

def teacher_head(inputs):
    query_rows, key_rows, value_rows = inputs
    scores = jnp.dot(query_rows.astype(jnp.float32), key_rows.T.astype(jnp.float32), preferred_element_type=jnp.float32) / math.sqrt(HD)
    position = jnp.arange(scores.shape[0])
    scores = jnp.where(position[None, :] <= position[:, None], scores, -jnp.inf)
    row_max = lax.optimization_barrier(jnp.max(scores, axis=1, keepdims=True))
    weights = jnp.exp(scores - row_max)
    mixed = jnp.dot(weights.astype(jnp.bfloat16).astype(jnp.float32), value_rows.astype(jnp.float32), preferred_element_type=jnp.float32)
    return (mixed / lax.optimization_barrier(jnp.sum(weights, axis=1, keepdims=True))).astype(jnp.bfloat16)

def reference(queries, key_heads, values, log_decay, write_strength, query_map, key_map, out_weight):
    group_size = QUERY_HEAD_COUNT // KVH
    query_split = queries.reshape(TOKEN_COUNT, QUERY_HEAD_COUNT, HD).transpose(1, 0, 2)
    key_split = jnp.repeat(key_heads.reshape(TOKEN_COUNT, KVH, HD).transpose(1, 0, 2), group_size, axis=0)
    value_split = jnp.repeat(values.reshape(TOKEN_COUNT, KVH, HD).transpose(1, 0, 2), group_size, axis=0)
    teacher = lax.map(teacher_head, (query_split, key_split, value_split))
    value_float = value_split.astype(jnp.float32)
    projected_query = jnp.einsum('htd,hde->hte', query_split.astype(jnp.float32), query_map.astype(jnp.float32), preferred_element_type=jnp.float32)
    projected_key = jnp.einsum('htd,hde->hte', key_split.astype(jnp.float32), key_map.astype(jnp.float32), preferred_element_type=jnp.float32)

    def student(proj_query, proj_key):
        start_state = jnp.zeros((QUERY_HEAD_COUNT, HD, HD), jnp.float32)
        last_state, outputs = run_spans(start_state, unit_rows(proj_query), unit_rows(proj_key), value_float, log_decay.T, write_strength.T, SPAN)
        return outputs
    student_out, pullback = jax.vjp(student, projected_query, projected_key)
    delta_heads = student_out - teacher.astype(jnp.float32)
    delta_rows = delta_heads.transpose(1, 0, 2).reshape(TOKEN_COUNT, QUERY_HEAD_COUNT * HD)
    weight_float = out_weight.astype(jnp.float32)
    difference = jnp.dot(delta_rows, weight_float, precision=BEST_PRECISION)
    mean_square = jnp.sum(difference * difference) / (TOKEN_COUNT * D)
    head_grad = jnp.dot(difference, weight_float.T, precision=BEST_PRECISION)
    head_grad = head_grad.reshape(TOKEN_COUNT, QUERY_HEAD_COUNT, HD).transpose(1, 0, 2)
    proj_query_grad, proj_key_grad = pullback(head_grad)
    query_grad = jnp.einsum('htd,hte->hde', query_split.astype(jnp.float32), proj_query_grad, precision=BEST_PRECISION)
    key_grad = jnp.einsum('htd,hte->hde', key_split.astype(jnp.float32), proj_key_grad, precision=BEST_PRECISION)
    return (mean_square, query_grad, key_grad)
```

```python
import functools
import math

import jax
import jax.numpy as jnp
from jax import lax
from jax.experimental import pallas as pl
from jax.experimental.pallas import tpu as pltpu
from jax.sharding import PartitionSpec as P

D = 8192
QUERY_HEAD_COUNT = 64
KVH = 8
HD = 128
ROWS = 512
BLK = 128
NB = ROWS // BLK
HEADS = 4
CTX = 8
CHIPS = 8
PIECE = 512
PAD = 16
SAME_CORE = [[2 * p + core for p in range(CHIPS)] for core in range(2)]

f32 = jnp.float32
bf16 = jnp.bfloat16
f16 = jnp.float16

VMEM_LIMIT = 56 * 1024 * 1024


def params():
    return pltpu.CompilerParams(vmem_limit_bytes=VMEM_LIMIT)


def split(x):
    high = x.astype(bf16)
    return high, (x - high.astype(f32)).astype(bf16)


NN = (((1,), (0,)), ((), ()))
NT = (((1,), (1,)), ((), ()))
TN = (((0,), (0,)), ((), ()))


def mm(a, b, dims):
    return lax.dot_general(a, b, dims, preferred_element_type=f32)


def mm3(a, b, dims):
    return mm(a[0], b[0], dims) + (mm(a[0], b[1], dims) + mm(a[1], b[0], dims))


def rows_of(pair, lo, hi):
    return pair[0][lo:hi], pair[1][lo:hi]


def stack(a, b):
    return jnp.concatenate([a[0], b[0]], axis=0), jnp.concatenate([a[1], b[1]], axis=0)


def unit(x):
    inverse = 1.0 / jnp.sqrt(jnp.sum(x * x, axis=-1, keepdims=True) + 1e-06)
    return x * inverse, inverse


def gate_forms(gates, writes, head):
    lane = lax.broadcasted_iota(jnp.int32, (ROWS, HEADS), 1)
    gate = jnp.sum(jnp.where(lane == head, gates, 0.0), axis=1, keepdims=True)
    write = jnp.sum(jnp.where(lane == head, writes, 0.0), axis=1, keepdims=True)
    ii = lax.broadcasted_iota(jnp.int32, (ROWS, ROWS), 0)
    jj = lax.broadcasted_iota(jnp.int32, (ROWS, ROWS), 1)
    gate_row = jnp.sum(jnp.where(ii == jj, gate, 0.0), axis=0, keepdims=True)
    column = jnp.sum(jnp.where(jj <= ii, gate_row, 0.0), axis=1, keepdims=True)
    row = jnp.sum(jnp.where(ii <= jj, gate, 0.0), axis=0, keepdims=True)
    return column, row, write


def decays(column, row, i):
    width = BLK * (i + 1)
    ii = lax.broadcasted_iota(jnp.int32, (BLK, width), 0) + BLK * i
    jj = lax.broadcasted_iota(jnp.int32, (BLK, width), 1)
    inclusive = ii >= jj
    gap = column[BLK * i : width] - row[:, :width]
    decay = jnp.where(inclusive, jnp.exp(jnp.where(inclusive, gap, 0.0)), 0.0)
    return decay, ii > jj


def inverses(blocks):
    ii = lax.broadcasted_iota(jnp.int32, (BLK, BLK), 0)
    jj = lax.broadcasted_iota(jnp.int32, (BLK, BLK), 1)
    diagonal = (ii == jj).astype(f32)
    first = ((ii >> 1) == (jj >> 1)) & (ii > jj)
    found = [diagonal - jnp.where(first, block, 0.0) for block in blocks]
    shift = 1
    while (1 << shift) < BLK:
        mask = ((ii >> (shift + 1)) == (jj >> (shift + 1))) & ((ii >> shift) > (jj >> shift))
        parts = [split(x) for x in found]
        corner = [split(jnp.where(mask, block, 0.0)) for block in blocks]
        inner = [split(mm3(c, x, NN)) for c, x in zip(corner, parts)]
        found = [x - mm3(p, y, NN) for x, p, y in zip(found, parts, inner)]
        shift += 1
    return found


def student_kernel(
    q_ref, k_ref, v_ref, gate_ref, write_ref, qmap_ref, kmap_ref,
    ah_ref, al_ref, lh_ref, ll_ref, dh_ref, dl_ref, x_ref, z_ref, message_ref,
):
    head = pl.program_id(0)
    column, row, write = gate_forms(gate_ref[...], write_ref[...], head)
    growth = jnp.exp(column)
    end = row[:, ROWS - 1 : ROWS]
    tail = jnp.exp(end - column)
    uq, _ = unit(mm(q_ref[...], qmap_ref[0], NN))
    uk, _ = unit(mm(k_ref[...], kmap_ref[0], NN))
    uqs, uks = split(uq), split(uk)
    lower, attend = [], []
    for i in range(NB):
        lo, hi = BLK * i, BLK * (i + 1)
        both = stack(rows_of(uks, lo, hi), rows_of(uqs, lo, hi))
        gram = mm3(both, rows_of(uks, 0, hi), NT)
        decay, strict = decays(column, row, i)
        lower.append(jnp.where(strict, gram[:BLK] * decay * write[lo:hi], 0.0))
        attend.append(gram[BLK:] * decay)
    inverse = [split(x) for x in inverses([lower[i][:, BLK * i :] for i in range(NB)])]
    right = jnp.concatenate([write * v_ref[...].astype(f32), (write * growth) * uk], axis=1)
    solved = None
    for i in range(NB):
        lo, hi = BLK * i, BLK * (i + 1)
        low = split(lower[i])
        lh_ref[0, lo:hi, :hi] = low[0]
        ll_ref[0, lo:hi, :hi] = low[1]
        dh_ref[0, lo:hi, :] = inverse[i][0]
        dl_ref[0, lo:hi, :] = inverse[i][1]
        rest = right[lo:hi]
        if i:
            rest = rest - mm3((low[0][:, :lo], low[1][:, :lo]), solved, NN)
        x = mm3(inverse[i], split(rest), NN)
        x_ref[0, lo:hi, :] = x
        solved = stack(solved, split(x)) if i else split(x)
    for i in range(NB):
        lo, hi = BLK * i, BLK * (i + 1)
        part = split(attend[i])
        ah_ref[0, lo:hi, :hi] = part[0]
        al_ref[0, lo:hi, :hi] = part[1]
        z = mm3(part, rows_of(solved, 0, hi), NN)
        z_ref[0, lo:hi, :HD] = z[:, :HD]
        z_ref[0, lo:hi, HD:] = growth[lo:hi] * uq[lo:hi] - z[:, HD:]
    moved = mm3(solved, split(tail * uk), TN)
    ii = lax.broadcasted_iota(jnp.int32, (HD, HD), 0)
    jj = lax.broadcasted_iota(jnp.int32, (HD, HD), 1)
    carry = jnp.where(ii == jj, jnp.exp(end), 0.0) - moved[HD:]
    half = HD // 2
    for s in range(2):
        message_ref[s, :half, :] = moved[half * s : half * (s + 1)]
        message_ref[s, half:, :] = carry


def student_local(queries, key_mine, value_mine, log_decay, write_strength, query_map, key_map):
    per_head = lambda *shape: pl.BlockSpec((1,) + shape, lambda h: (h,) + (0,) * len(shape))
    whole = lambda *shape: pl.BlockSpec(shape, lambda h: (0,) * len(shape))
    square = jax.ShapeDtypeStruct((HEADS, ROWS, ROWS), bf16)
    narrow = jax.ShapeDtypeStruct((HEADS, ROWS, BLK), bf16)
    wide = jax.ShapeDtypeStruct((HEADS, ROWS, 2 * HD), f32)
    return pl.pallas_call(
        student_kernel,
        grid=(HEADS,),
        in_specs=[
            pl.BlockSpec((ROWS, HD), lambda h: (0, h)),
            whole(ROWS, HD),
            whole(ROWS, HD),
            whole(ROWS, HEADS),
            whole(ROWS, HEADS),
            per_head(HD, HD),
            per_head(HD, HD),
        ],
        out_specs=[
            per_head(ROWS, ROWS),
            per_head(ROWS, ROWS),
            per_head(ROWS, ROWS),
            per_head(ROWS, ROWS),
            per_head(ROWS, BLK),
            per_head(ROWS, BLK),
            per_head(ROWS, 2 * HD),
            per_head(ROWS, 2 * HD),
            pl.BlockSpec((2, HD + HD // 2, HD), lambda h: (h, 0, 0)),
        ],
        out_shape=[
            square, square, square, square, narrow, narrow, wide, wide,
            jax.ShapeDtypeStruct((2 * HEADS, HD + HD // 2, HD), f32),
        ],
        compiler_params=params(),
        name="student_local",
    )(queries, key_mine, value_mine, log_decay, write_strength, query_map, key_map)


def chain_kernel(message_ref, out_ref):
    half = HD // 2
    state = jnp.zeros((half, HD), f32)
    out_ref[0] = state
    for c in range(CTX - 1):
        carry = split(message_ref[c, half:, :])
        state = mm3(split(state), carry, NN) + message_ref[c, :half, :]
        out_ref[c + 1] = state


def chain(messages):
    return pl.pallas_call(
        chain_kernel,
        out_shape=jax.ShapeDtypeStruct((CTX, HD // 2, HD), f32),
        compiler_params=params(),
        name="state_chain",
    )(messages)


def back_chain_kernel(message_ref, grad_ref, out_ref):
    half = HD // 2
    state = jnp.zeros((half, HD), f32)
    out_ref[CTX - 1] = state
    for c in range(CTX - 1, 0, -1):
        carry = split(message_ref[c, half:, :])
        state = mm3(split(state), carry, NT) + grad_ref[c]
        out_ref[c - 1] = state


def back_chain(messages, grads):
    return pl.pallas_call(
        back_chain_kernel,
        out_shape=jax.ShapeDtypeStruct((CTX, HD // 2, HD), f32),
        compiler_params=params(),
        name="state_grad_chain",
    )(messages, grads)


def teacher_kernel(ctx_ref, q_ref, kv_ref, z_ref, state_ref, high_ref, low_ref):
    mine = ctx_ref[0]
    q = q_ref[...]
    scale = 1.0 / math.sqrt(HD)

    def block(j, carry, diagonal):
        top, total, mixed = carry
        start = pl.multiple_of(j * ROWS, ROWS)
        keys = kv_ref[pl.ds(start, ROWS), :HD]
        values = kv_ref[pl.ds(start, ROWS), HD:]
        scores = mm(q, keys, NT) * scale
        if diagonal:
            ii = lax.broadcasted_iota(jnp.int32, (ROWS, ROWS), 0)
            jj = lax.broadcasted_iota(jnp.int32, (ROWS, ROWS), 1)
            scores = jnp.where(jj <= ii, scores, -jnp.inf)
        new_top = jnp.maximum(top, jnp.max(scores, axis=1, keepdims=True))
        fade = jnp.exp(top - new_top)
        weights = jnp.exp(scores - new_top)
        total = total * fade + jnp.sum(weights, axis=1, keepdims=True)
        mixed = mixed * fade + mm(weights.astype(bf16), values, NN)
        return new_top, total, mixed

    start = (
        jnp.full((ROWS, 1), -jnp.inf, f32),
        jnp.zeros((ROWS, 1), f32),
        jnp.zeros((ROWS, HD), f32),
    )
    carry = block(mine, start, True)
    _, total, mixed = lax.fori_loop(0, mine, lambda j, c: block(j, c, False), carry)
    teacher = (mixed / total).astype(bf16).astype(f32)
    student = z_ref[0, :, :HD] + mm3(split(z_ref[0, :, HD:]), split(state_ref[0]), NT)
    delta = split(student - teacher)
    high_ref[...] = delta[0]
    low_ref[...] = delta[1]


def teacher_delta(ctx, queries, kv, z, state):
    return pl.pallas_call(
        teacher_kernel,
        grid_spec=pltpu.PrefetchScalarGridSpec(
            num_scalar_prefetch=1,
            grid=(HEADS,),
            in_specs=[
                pl.BlockSpec((ROWS, HD), lambda h, c: (0, h)),
                pl.BlockSpec((CTX * ROWS, 2 * HD), lambda h, c: (0, 0)),
                pl.BlockSpec((1, ROWS, 2 * HD), lambda h, c: (h, 0, 0)),
                pl.BlockSpec((1, HD, HD), lambda h, c: (h, 0, 0)),
            ],
            out_specs=[
                pl.BlockSpec((ROWS, HD), lambda h, c: (0, h)),
                pl.BlockSpec((ROWS, HD), lambda h, c: (0, h)),
            ],
        ),
        out_shape=[jax.ShapeDtypeStruct((ROWS, HEADS * HD), bf16)] * 2,
        compiler_params=params(),
        name="teacher_delta",
    )(ctx, queries, kv, z, state)


def project_kernel(core_ref, mine_ref, other_ref, w_mine_ref, w_other_ref, out_ref):
    width = HEADS * HD
    total = mm(mine_ref[:, width:], w_mine_ref[...], NN)
    total = total + mm(other_ref[:, width:], w_other_ref[...], NN)
    total = total + mm(mine_ref[:, :width], w_mine_ref[...], NN)
    total = total + mm(other_ref[:, :width], w_other_ref[...], NN)
    out_ref[0] = total


def project(core, mine, other, w_mine, w_other):
    width = HEADS * HD
    return pl.pallas_call(
        project_kernel,
        grid_spec=pltpu.PrefetchScalarGridSpec(
            num_scalar_prefetch=1,
            grid=(CHIPS,),
            in_specs=[
                pl.BlockSpec((ROWS, 2 * width), lambda j, c: (0, 0)),
                pl.BlockSpec((ROWS, 2 * width), lambda j, c: (0, 0)),
                pl.BlockSpec((width, PIECE), lambda j, c: (0, c[0] * CHIPS + j)),
                pl.BlockSpec((width, PIECE), lambda j, c: (0, j)),
            ],
            out_specs=pl.BlockSpec((1, ROWS, PIECE), lambda j, c: (j, 0, 0)),
        ),
        out_shape=jax.ShapeDtypeStruct((CHIPS, ROWS, PIECE), f32),
        compiler_params=params(),
        name="difference_part",
    )(core, mine, other, w_mine, w_other)


def back_project_kernel(core_ref, high_ref, low_ref, w_mine_ref, w_other_ref, mine_ref, other_ref):
    mine = mm(high_ref[0], w_mine_ref[...], NT) + mm(low_ref[0], w_mine_ref[...], NT)
    other = mm(high_ref[0], w_other_ref[...], NT) + mm(low_ref[0], w_other_ref[...], NT)

    @pl.when(pl.program_id(0) == 0)
    def _():
        mine_ref[...] = mine
        other_ref[...] = other

    @pl.when(pl.program_id(0) > 0)
    def _():
        mine_ref[...] += mine
        other_ref[...] += other


def back_project(core, high, low, w_mine, w_other):
    width = HEADS * HD
    return pl.pallas_call(
        back_project_kernel,
        grid_spec=pltpu.PrefetchScalarGridSpec(
            num_scalar_prefetch=1,
            grid=(CHIPS,),
            in_specs=[
                pl.BlockSpec((1, ROWS, PIECE), lambda j, c: (j, 0, 0)),
                pl.BlockSpec((1, ROWS, PIECE), lambda j, c: (j, 0, 0)),
                pl.BlockSpec((width, PIECE), lambda j, c: (0, c[0] * CHIPS + j)),
                pl.BlockSpec((width, PIECE), lambda j, c: (0, j)),
            ],
            out_specs=[pl.BlockSpec((ROWS, width), lambda j, c: (0, 0))] * 2,
        ),
        out_shape=[jax.ShapeDtypeStruct((ROWS, width), f32)] * 2,
        compiler_params=params(),
        name="head_grad_part",
    )(core, high, low, w_mine, w_other)


def state_grad_kernel(grad_ref, z_ref, out_ref):
    out_ref[0] = mm3(split(grad_ref[...]), split(z_ref[0, :, HD:]), TN)


def state_grad_local(head_grad, z):
    return pl.pallas_call(
        state_grad_kernel,
        grid=(HEADS,),
        in_specs=[
            pl.BlockSpec((ROWS, HD), lambda h: (0, h)),
            pl.BlockSpec((1, ROWS, 2 * HD), lambda h: (h, 0, 0)),
        ],
        out_specs=pl.BlockSpec((1, HD, HD), lambda h: (h, 0, 0)),
        out_shape=jax.ShapeDtypeStruct((HEADS, HD, HD), f32),
        compiler_params=params(),
        name="state_grad_local",
    )(head_grad, z)


def backward_kernel(
    q_ref, k_ref, gate_ref, write_ref, qmap_ref, kmap_ref,
    ah_ref, al_ref, lh_ref, ll_ref, dh_ref, dl_ref, x_ref,
    state_ref, grad_ref, state_grad_ref,
    qgrad_ref, kgrad_ref,
):
    head = pl.program_id(0)
    column, row, write = gate_forms(gate_ref[...], write_ref[...], head)
    growth = jnp.exp(column)
    tail = jnp.exp(row[:, ROWS - 1 : ROWS] - column)
    uq, q_inverse = unit(mm(q_ref[...], qmap_ref[0], NN))
    uk, k_inverse = unit(mm(k_ref[...], kmap_ref[0], NN))
    uqs, uks = split(uq), split(uk)
    state = split(state_ref[0])
    state_grad = split(state_grad_ref[0])
    grad = split(grad_ref[...])
    x = x_ref[0]
    updates = split(x[:, :HD] - mm3(split(x[:, HD:]), state, NT))
    reach = mm3(split(tail * uk), state_grad, NT)
    right = [None] * NB
    for j in range(NB):
        lo, hi = BLK * j, BLK * (j + 1)
        part = (ah_ref[0, lo:, lo:hi], al_ref[0, lo:, lo:hi])
        right[j] = mm3(part, rows_of(grad, lo, ROWS), TN) + reach[lo:hi]
    solved = None
    for j in range(NB - 1, -1, -1):
        lo, hi = BLK * j, BLK * (j + 1)
        rest = right[j]
        if solved is not None:
            part = (lh_ref[0, hi:, lo:hi], ll_ref[0, hi:, lo:hi])
            rest = rest - mm3(part, solved, TN)
        y = split(mm3((dh_ref[0, lo:hi, :], dl_ref[0, lo:hi, :]), split(rest), TN))
        solved = y if solved is None else stack(y, solved)
    key_total = [None] * NB
    query_total = []
    from_state = mm3(stack(grad, solved), state, NN)
    from_next = mm3(updates, state_grad, NN)
    for i in range(NB - 1, -1, -1):
        lo, hi = BLK * i, BLK * (i + 1)
        pair = stack(rows_of(grad, lo, hi), rows_of(solved, lo, hi))
        outer = mm3(pair, rows_of(updates, 0, hi), NT)
        decay, strict = decays(column, row, i)
        through = jnp.concatenate(
            [outer[:BLK] * decay, jnp.where(strict, -outer[BLK:] * decay * write[lo:hi], 0.0)],
            axis=0,
        )
        through = split(through)
        rows = mm3(through, rows_of(uks, 0, hi), NN)
        query_total.append(growth[lo:hi] * from_state[lo:hi] + rows[:BLK])
        columns = mm3(through, stack(rows_of(uqs, lo, hi), rows_of(uks, lo, hi)), TN)
        own = rows[BLK:] + tail[lo:hi] * from_next[lo:hi]
        own = own - (write[lo:hi] * growth[lo:hi]) * from_state[ROWS + lo : ROWS + hi]
        for j in range(i + 1):
            more = columns[BLK * j : BLK * (j + 1)]
            if j == i:
                more = more + own
            key_total[j] = more if key_total[j] is None else key_total[j] + more
    query_grad = jnp.concatenate(query_total[::-1], axis=0)
    key_grad = jnp.concatenate(key_total, axis=0)
    query_grad = q_inverse * (query_grad - uq * jnp.sum(uq * query_grad, axis=1, keepdims=True))
    key_grad = k_inverse * (key_grad - uk * jnp.sum(uk * key_grad, axis=1, keepdims=True))
    query_grad, key_grad = split(query_grad), split(key_grad)
    q, k = q_ref[...], k_ref[...]
    qgrad_ref[0] = mm(q, query_grad[0], TN) + mm(q, query_grad[1], TN)
    kgrad_ref[0] = mm(k, key_grad[0], TN) + mm(k, key_grad[1], TN)


def backward_local(
    queries, key_mine, log_decay, write_strength, query_map, key_map, kept, state, head_grad, state_grad
):
    per_head = lambda *shape: pl.BlockSpec((1,) + shape, lambda h: (h,) + (0,) * len(shape))
    whole = lambda *shape: pl.BlockSpec(shape, lambda h: (0,) * len(shape))
    column = pl.BlockSpec((ROWS, HD), lambda h: (0, h))
    return pl.pallas_call(
        backward_kernel,
        grid=(HEADS,),
        in_specs=[
            column,
            whole(ROWS, HD),
            whole(ROWS, HEADS),
            whole(ROWS, HEADS),
            per_head(HD, HD),
            per_head(HD, HD),
            per_head(ROWS, ROWS),
            per_head(ROWS, ROWS),
            per_head(ROWS, ROWS),
            per_head(ROWS, ROWS),
            per_head(ROWS, BLK),
            per_head(ROWS, BLK),
            per_head(ROWS, 2 * HD),
            per_head(HD, HD),
            column,
            per_head(HD, HD),
        ],
        out_specs=[per_head(HD, HD), per_head(HD, HD)],
        out_shape=[jax.ShapeDtypeStruct((HEADS, HD, HD), f32)] * 2,
        compiler_params=params(),
        name="student_backward",
    )(
        queries, key_mine, log_decay, write_strength, query_map, key_map,
        *kept, state, head_grad, state_grad,
    )


def exponent_for(x):
    largest = jnp.maximum(jnp.max(jnp.abs(x)), 1e-30)
    return jnp.clip(14.0 - jnp.ceil(jnp.log2(largest)), -100.0, 100.0)


def packed(x):
    exponent = exponent_for(x)
    body = (x * jnp.exp2(exponent)).astype(f16)
    extra = jnp.broadcast_to(exponent.astype(f16), x.shape[:-2] + (PAD, x.shape[-1]))
    return jnp.concatenate([body, extra], axis=-2)


def unpacked(message):
    exponent = message[..., -1:, :].astype(f32)
    return message[..., :-PAD, :].astype(f32) * jnp.exp2(-exponent)


def transpose_over(x, axis, groups=None):
    return lax.all_to_all(x, axis, 0, 0, axis_index_groups=groups, tiled=True)


def shards(queries, key_heads, values, log_decay, write_strength, query_map, key_map, out_weight):
    ctx = lax.axis_index("ctx")
    head_index = lax.axis_index("head")
    core = lax.rem(head_index, 2)
    kv_column = head_index * HEADS // (QUERY_HEAD_COUNT // KVH) * HD
    key_mine = lax.dynamic_slice_in_dim(key_heads, kv_column, HD, 1)
    value_mine = lax.dynamic_slice_in_dim(values, kv_column, HD, 1)
    kv = lax.all_gather(
        jnp.concatenate([key_mine, value_mine], axis=1), "ctx", axis=0, tiled=True
    )
    partner = [(i, i ^ 1) for i in range(2 * CHIPS)]
    half = D // 2
    w_other = lax.ppermute(
        lax.dynamic_slice_in_dim(out_weight, (1 - core) * half, half, 1), "head", partner
    )
    *kept, z, message = student_local(
        queries, key_mine, value_mine, log_decay, write_strength, query_map, key_map
    )
    messages = transpose_over(message, "ctx")
    state = transpose_over(chain(messages), "ctx").reshape(HEADS, HD, HD)
    ctx_scalar = ctx.astype(jnp.int32).reshape(1)
    core_scalar = core.astype(jnp.int32).reshape(1)
    high, low = teacher_delta(ctx_scalar, queries, kv, z, state)
    delta = jnp.concatenate([high, low], axis=1)
    delta_other = lax.ppermute(delta, "head", partner)
    part = project(core_scalar, delta, delta_other, out_weight, w_other)
    pieces = transpose_over(packed(part), "head", SAME_CORE)
    difference = jnp.sum(unpacked(pieces), axis=0)
    gathered = lax.all_gather(
        packed(difference), "head", axis=0, axis_index_groups=SAME_CORE, tiled=False
    )
    columns = unpacked(gathered)
    square_mine = jnp.broadcast_to(jnp.sum(columns * columns), (8, HD))
    square_other = lax.ppermute(square_mine, "head", partner)
    columns_high, columns_low = split(columns)
    grad_mine, grad_other = back_project(
        core_scalar, columns_high, columns_low, out_weight, w_other
    )
    head_grad = grad_mine + lax.ppermute(grad_other, "head", partner)
    local = state_grad_local(head_grad, z).reshape(CTX, HD // 2, HD)
    locals_ = transpose_over(local, "ctx")
    state_grad = transpose_over(back_chain(messages, locals_), "ctx").reshape(HEADS, HD, HD)
    query_grad, key_grad = backward_local(
        queries, key_mine, log_decay, write_strength, query_map, key_map,
        kept, state, head_grad, state_grad,
    )
    grads = jnp.concatenate([query_grad, key_grad], axis=0)
    extra = jnp.broadcast_to(square_mine + square_other, (2 * HEADS, 8, HD))
    shared = transpose_over(jnp.concatenate([grads, extra], axis=1), "ctx")
    total = jnp.sum(shared, axis=0, keepdims=True)
    final = transpose_over(jnp.broadcast_to(total, (CTX,) + total.shape[1:]), "ctx")
    normalizer = CTX * ROWS * D
    return final[0, HD, 0] / normalizer, final[:HEADS, :HD], final[HEADS:, :HD]


def solution(mesh):
    placed = (
        P("ctx", "head"),
        P("ctx", None),
        P("ctx", None),
        P("ctx", "head"),
        P("ctx", "head"),
        P("head", None, None),
        P("head", None, None),
        P("head", None),
    )
    return jax.shard_map(
        shards,
        mesh=mesh,
        in_specs=placed,
        out_specs=(P(), P("head", None, None), P("head", None, None)),
        check_vma=False,
    )
```

```python
import functools
import math

import jax
import jax.numpy as jnp
from jax import lax
from jax.experimental import pallas as pl
from jax.experimental.pallas import tpu as pltpu
from jax.sharding import PartitionSpec as P

D = 8192
QUERY_HEAD_COUNT = 64
KVH = 8
HD = 128
ROWS = 512
BLK = 128
NB = ROWS // BLK
TRI = (2 * BLK, 5 * BLK)
HEADS = 4
CTX = 8
CHIPS = 8
PIECE = 512
PAD = 16
SAME_CORE = [[2 * p + core for p in range(CHIPS)] for core in range(2)]

f32 = jnp.float32
bf16 = jnp.bfloat16
f16 = jnp.float16

MIB = 1024 * 1024
FLOOR = 0
PROJECT_MIB = 24
BACK_MIB = 40
PSTEP = 2
STEP = 1
HALF = ROWS // 2
KSTEP = 4
DSTEP = 2
TEACH = 4


def params(mib):
    return pltpu.CompilerParams(vmem_limit_bytes=max(mib, FLOOR) * MIB)


def cost(micros):
    return pl.CostEstimate(flops=int(micros * 1.1e9), bytes_accessed=0, transcendentals=0)


def split(x):
    high = x.astype(bf16)
    return high, (x - high.astype(f32)).astype(bf16)


NN = (((1,), (0,)), ((), ()))
NT = (((1,), (1,)), ((), ()))
TN = (((0,), (0,)), ((), ()))


def mm(a, b, dims):
    return lax.dot_general(a, b, dims, preferred_element_type=f32)


def beside(a, b):
    return jnp.concatenate([a, b], axis=1)


def above(a, b):
    return jnp.concatenate([a, b], axis=0)


def halves(x):
    n = x.shape[1] // 2
    return x[:, :n] + x[:, n:]


def mm3(a, b, dims):
    depth_at = dims[0][0][0]
    depth = a[0].shape[depth_at]
    if depth <= 128:
        left = beside(*a) if depth_at == 1 else above(*a)
        if dims is NT:
            return halves(mm(left, above(beside(b[0], b[0]), beside(b[1], b[1])), dims))
        if b[0].shape[1] <= 128:
            wide = beside(*b)
            return halves(mm(left, above(wide, wide), dims))
        return mm(left, above(b[0], b[0]), dims) + mm(a[0], b[1], dims)
    if dims is not NT and b[0].shape[1] <= 128:
        return halves(mm(a[0], beside(*b), dims)) + mm(a[1], b[0], dims)
    return mm(a[0], b[0], dims) + (mm(a[0], b[1], dims) + mm(a[1], b[0], dims))


def rows_of(pair, lo, hi):
    return pair[0][lo:hi], pair[1][lo:hi]


def stack(a, b):
    return above(a[0], b[0]), above(a[1], b[1])


PACKED = ((0, 4 * BLK), (BLK, 3 * BLK), (BLK, 0), (0, 0))


def block(refs, n, i, j):
    at, left = PACKED[i]
    return tuple(ref[n, at : at + BLK, left + BLK * j : left + BLK * (j + 1)] for ref in refs)


def block_column(refs, n, j, first):
    parts = []
    for ref in refs:
        blocks = []
        for i in range(first, NB):
            at, left = PACKED[i]
            blocks.append(ref[n, at : at + BLK, left + BLK * j : left + BLK * (j + 1)])
        parts.append(jnp.concatenate(blocks, axis=0))
    return tuple(parts)


def store_row(refs, n, i, pair):
    at, left = PACKED[i]
    for ref, part in zip(refs, pair):
        ref[n, at : at + BLK, left : left + BLK * (i + 1)] = part


def loaded(refs, n):
    return refs[0][n], refs[1][n]


def store(refs, n, pair):
    refs[0][n] = pair[0]
    refs[1][n] = pair[1]


def unit(x):
    inverse = 1.0 / jnp.sqrt(jnp.sum(x * x, axis=-1, keepdims=True) + 1e-06)
    return x * inverse, inverse


def through_unit(grad, units, inverse):
    return inverse * (grad - units * jnp.sum(units * grad, axis=1, keepdims=True))


def gate_forms(gate_row, write_row):
    ii = lax.broadcasted_iota(jnp.int32, (ROWS, ROWS), 0)
    jj = lax.broadcasted_iota(jnp.int32, (ROWS, ROWS), 1)
    gate = jnp.sum(jnp.where(ii == jj, gate_row, 0.0), axis=1, keepdims=True)
    write = jnp.sum(jnp.where(ii == jj, write_row, 0.0), axis=1, keepdims=True)
    column = jnp.sum(jnp.where(jj <= ii, gate_row, 0.0), axis=1, keepdims=True)
    row = jnp.sum(jnp.where(ii <= jj, gate, 0.0), axis=0, keepdims=True)
    return column, row, write


def decays(column, row, i):
    width = BLK * (i + 1)
    ii = lax.broadcasted_iota(jnp.int32, (BLK, width), 0) + BLK * i
    jj = lax.broadcasted_iota(jnp.int32, (BLK, width), 1)
    inclusive = ii >= jj
    gap = column[BLK * i : width] - row[:, :width]
    return jnp.where(inclusive, jnp.exp(jnp.where(inclusive, gap, 0.0)), 0.0)


def strict(i):
    width = BLK * (i + 1)
    ii = lax.broadcasted_iota(jnp.int32, (BLK, width), 0) + BLK * i
    return ii > lax.broadcasted_iota(jnp.int32, (BLK, width), 1)


def inverses(blocks):
    ii = lax.broadcasted_iota(jnp.int32, (BLK, BLK), 0)
    jj = lax.broadcasted_iota(jnp.int32, (BLK, BLK), 1)
    diagonal = (ii == jj).astype(f32)
    first = ((ii >> 1) == (jj >> 1)) & (ii > jj)
    found = [diagonal - jnp.where(first, block, 0.0) for block in blocks]
    whole_parts = [split(block) for block in blocks]
    none = jnp.zeros((BLK, BLK), bf16)
    shift = 1
    while (1 << shift) < BLK:
        mask = ((ii >> (shift + 1)) == (jj >> (shift + 1))) & ((ii >> shift) > (jj >> shift))
        parts = [split(x) for x in found]
        corner = [tuple(jnp.where(mask, part, none) for part in pair) for pair in whole_parts]
        inner = [split(mm3(c, x, NN)) for c, x in zip(corner, parts)]
        found = [x - mm3(p, y, NN) for x, p, y in zip(found, parts, inner)]
        shift += 1
    return found


GROWTH, TAIL, WRITE, WRITE_GROWTH, INVERSE, COLUMN = range(6)


def column_of(ref, n, which):
    return ref[n, :, which : which + 1]


def per_head(*shape, step=None):
    return pl.BlockSpec((step or STEP,) + shape, lambda h, *_: (h,) + (0,) * len(shape))


def whole(*shape):
    return pl.BlockSpec(shape, lambda h, *_: (0,) * len(shape))


def columns_spec(step=None):
    return pl.BlockSpec((ROWS, (step or STEP) * HD), lambda h, *_: (0, h))


def pair_shape(*shape):
    return [jax.ShapeDtypeStruct((HEADS,) + shape, bf16)] * 2


def heads_call(kernel, name, micros, in_specs, out_specs, out_shape, mib=56, step=None):
    return pl.pallas_call(
        kernel,
        grid=(HEADS // (step or STEP),),
        in_specs=in_specs,
        out_specs=out_specs,
        out_shape=out_shape,
        compiler_params=params(mib),
        cost_estimate=cost(micros),
        name=name,
    )


def keys_kernel(
    k_ref, v_ref, gate_ref, write_ref, kmap_ref,
    cols_ref, row_ref, ukh_ref, ukl_ref, lh_ref, ll_ref, dh_ref, dl_ref, xh_ref, xl_ref, message_ref,
):
    heads = range(KSTEP)
    lower, uks, columns, rights, ends = [], [], [], [], []
    for n in heads:
        column, row, write = gate_forms(
            gate_ref[pl.ds(pl.program_id(0) * KSTEP + n, 1), :],
            write_ref[pl.ds(pl.program_id(0) * KSTEP + n, 1), :],
        )
        end = row[:, ROWS - 1 : ROWS]
        growth = jnp.exp(column)
        tail = jnp.exp(end - column)
        uk, inverse = unit(mm(k_ref[...], kmap_ref[n], NN))
        pair = split(uk)
        store((ukh_ref, ukl_ref), n, pair)
        for which, value in enumerate((growth, tail, write, write * growth, inverse, column)):
            cols_ref[n, :, which : which + 1] = value
        row_ref[n] = row
        own = []
        for i in range(NB):
            lo, hi = BLK * i, BLK * (i + 1)
            gram = mm3(rows_of(pair, lo, hi), rows_of(pair, 0, hi), NT)
            decay = decays(column, row, i)
            own.append(jnp.where(strict(i), gram * decay * write[lo:hi], 0.0))
        lower.append(own)
        uks.append(split(tail * uk))
        rights.append(beside(write * v_ref[...].astype(f32), (write * growth) * uk))
        ends.append(end)
    found = inverses([lower[n][i][:, BLK * i :] for n in heads for i in range(NB)])
    inverse = [[split(found[n * NB + i]) for i in range(NB)] for n in heads]
    solved = [None] * KSTEP
    for i in range(NB):
        lo, hi = BLK * i, BLK * (i + 1)
        for n in heads:
            low = split(lower[n][i])
            store_row((lh_ref, ll_ref), n, i, low)
            dh_ref[n, lo:hi, :] = inverse[n][i][0]
            dl_ref[n, lo:hi, :] = inverse[n][i][1]
            rest = rights[n][lo:hi]
            if i:
                rest = rest - mm3((low[0][:, :lo], low[1][:, :lo]), solved[n], NN)
            x = split(mm3(inverse[n][i], split(rest), NN))
            solved[n] = stack(solved[n], x) if i else x
    ii = lax.broadcasted_iota(jnp.int32, (HD, HD), 0)
    jj = lax.broadcasted_iota(jnp.int32, (HD, HD), 1)
    half = HD // 2
    for n in heads:
        store((xh_ref, xl_ref), n, solved[n])
        moved = mm3(solved[n], uks[n], TN)
        carry = jnp.where(ii == jj, jnp.exp(ends[n]), 0.0) - moved[HD:]
        for s in range(2):
            message_ref[2 * n + s, :half, :] = moved[half * s : half * (s + 1)]
            message_ref[2 * n + s, half:, :] = carry


def student_keys(key_mine, value_mine, log_decay, write_strength, key_map):
    return heads_call(
        keys_kernel, "student_keys", 16,
        [whole(ROWS, HD), whole(ROWS, HD), whole(HEADS, ROWS), whole(HEADS, ROWS), per_head(HD, HD, step=KSTEP)],
        [
            per_head(ROWS, 8, step=KSTEP), per_head(1, ROWS, step=KSTEP),
            per_head(ROWS, HD, step=KSTEP), per_head(ROWS, HD, step=KSTEP),
            per_head(*TRI, step=KSTEP), per_head(*TRI, step=KSTEP),
            per_head(ROWS, BLK, step=KSTEP), per_head(ROWS, BLK, step=KSTEP),
            per_head(ROWS, 2 * HD, step=KSTEP), per_head(ROWS, 2 * HD, step=KSTEP),
            pl.BlockSpec((2 * KSTEP, HD + HD // 2, HD), lambda h: (h, 0, 0)),
        ],
        [
            jax.ShapeDtypeStruct((HEADS, ROWS, 8), f32),
            jax.ShapeDtypeStruct((HEADS, 1, ROWS), f32),
            *pair_shape(ROWS, HD), *pair_shape(*TRI), *pair_shape(ROWS, BLK), *pair_shape(ROWS, 2 * HD),
            jax.ShapeDtypeStruct((2 * HEADS, HD + HD // 2, HD), f32),
        ],
        step=KSTEP,
    )(key_mine, value_mine, log_decay.T, write_strength.T, key_map)


def queries_kernel(
    q_ref, qmap_ref, cols_ref, row_ref, ukh_ref, ukl_ref, xh_ref, xl_ref,
    inverse_ref, uqh_ref, uql_ref, ah_ref, al_ref, own_ref, rh_ref, rl_ref,
):
    for n in range(STEP):
        uq, inverse = unit(mm(q_ref[:, HD * n : HD * (n + 1)], qmap_ref[n], NN))
        inverse_ref[n, :, :1] = inverse
        uqs = split(uq)
        store((uqh_ref, uql_ref), n, uqs)
        uks = loaded((ukh_ref, ukl_ref), n)
        solved = loaded((xh_ref, xl_ref), n)
        reach = column_of(cols_ref, n, GROWTH) * uq
        for i in range(NB):
            lo, hi = BLK * i, BLK * (i + 1)
            decay = decays(column_of(cols_ref, n, COLUMN), row_ref[n], i)
            attend = split(mm3(rows_of(uqs, lo, hi), rows_of(uks, 0, hi), NT) * decay)
            store_row((ah_ref, al_ref), n, i, attend)
            z = mm3(attend, rows_of(solved, 0, hi), NN)
            own_ref[n, lo:hi, :] = z[:, :HD]
            part = split(reach[lo:hi] - z[:, HD:])
            rh_ref[n, lo:hi, :] = part[0]
            rl_ref[n, lo:hi, :] = part[1]


def student_queries(queries, query_map, cols, row, uk, solved):
    return heads_call(
        queries_kernel, "student_queries", 8,
        [
            columns_spec(), per_head(HD, HD), per_head(ROWS, 8), per_head(1, ROWS),
            per_head(ROWS, HD), per_head(ROWS, HD), per_head(ROWS, 2 * HD), per_head(ROWS, 2 * HD),
        ],
        [
            per_head(ROWS, 8), per_head(ROWS, HD), per_head(ROWS, HD), per_head(*TRI),
            per_head(*TRI), per_head(ROWS, HD), per_head(ROWS, HD), per_head(ROWS, HD),
        ],
        [
            jax.ShapeDtypeStruct((HEADS, ROWS, 8), f32),
            *pair_shape(ROWS, HD), *pair_shape(*TRI),
            jax.ShapeDtypeStruct((HEADS, ROWS, HD), f32),
            *pair_shape(ROWS, HD),
        ],
    )(queries, query_map, cols, row, *uk, *solved)


def chain_kernel(message_ref, out_ref):
    half = HD // 2
    carries = [split(message_ref[c, half:, :]) for c in range(CTX - 1)]
    state = jnp.zeros((half, HD), f32)
    out_ref[0] = state
    for c in range(CTX - 1):
        state = mm3(split(state), carries[c], NN) + message_ref[c, :half, :]
        out_ref[c + 1] = state


def chain(messages):
    return pl.pallas_call(
        chain_kernel,
        out_shape=jax.ShapeDtypeStruct((CTX, HD // 2, HD), f32),
        compiler_params=params(8),
        cost_estimate=cost(3),
        name="state_chain",
    )(messages)


def back_chain_kernel(message_ref, grad_ref, out_ref):
    half = HD // 2
    carries = [split(message_ref[c, half:, :]) for c in range(CTX)]
    state = jnp.zeros((half, HD), f32)
    out_ref[CTX - 1] = state
    for c in range(CTX - 1, 0, -1):
        state = mm3(split(state), carries[c], NT) + grad_ref[c]
        out_ref[c - 1] = state


def back_chain(messages, grads):
    return pl.pallas_call(
        back_chain_kernel,
        out_shape=jax.ShapeDtypeStruct((CTX, HD // 2, HD), f32),
        compiler_params=params(8),
        cost_estimate=cost(3),
        name="state_grad_chain",
    )(messages, grads)


def teacher_kernel(half, ctx_ref, q_ref, kv_ref, out_ref):
    mine = ctx_ref[0]
    scale = math.log2(math.e) / math.sqrt(HD)

    def block(j, carry, width, diagonal):
        start = pl.multiple_of(j * ROWS, ROWS)
        keys = kv_ref[pl.ds(start, width), :HD]
        values = kv_ref[pl.ds(start, width), HD:]
        out = []
        raw = [mm(q_ref[:, HD * n : HD * (n + 1)], keys, NT) for n in range(TEACH)]
        for n in range(TEACH):
            top, total, mixed = carry[n]
            scores = raw[n]
            if diagonal:
                ii = lax.broadcasted_iota(jnp.int32, (HALF, width), 0) + HALF * half
                jj = lax.broadcasted_iota(jnp.int32, (HALF, width), 1)
                scores = jnp.where(jj <= ii, scores, -jnp.inf)
            new_top = jnp.maximum(top, jnp.max(scores, axis=1, keepdims=True))
            fade = jnp.exp2((top - new_top) * scale)
            weights = jnp.exp2((scores - new_top) * scale)
            total = total * fade + jnp.sum(weights, axis=1, keepdims=True)
            mixed = mixed * fade + mm(weights.astype(bf16), values, NN)
            out.append((new_top, total, mixed))
        return tuple(out)

    start = (
        jnp.full((HALF, 1), -jnp.inf, f32),
        jnp.zeros((HALF, 1), f32),
        jnp.zeros((HALF, HD), f32),
    )
    carry = block(mine, (start,) * TEACH, HALF * (half + 1), True)
    carry = lax.fori_loop(0, mine, lambda j, c: block(j, c, ROWS, False), carry)
    for n in range(TEACH):
        _, total, mixed = carry[n]
        out_ref[:, HD * n : HD * (n + 1)] = (mixed / total).astype(bf16)


def teacher_out(half, ctx, queries, kv):
    return pl.pallas_call(
        functools.partial(teacher_kernel, half),
        grid_spec=pltpu.PrefetchScalarGridSpec(
            num_scalar_prefetch=1,
            grid=(HEADS // TEACH,),
            in_specs=[
                pl.BlockSpec((HALF, TEACH * HD), lambda h, c: (half, h)),
                pl.BlockSpec((CTX * ROWS, 2 * HD), lambda h, c: (0, 0)),
            ],
            out_specs=pl.BlockSpec((HALF, TEACH * HD), lambda h, c: (0, h)),
        ),
        out_shape=jax.ShapeDtypeStruct((HALF, HEADS * HD), bf16),
        compiler_params=params(24),
        cost_estimate=cost(9),
        name=f"teacher_{half}",
    )(ctx, queries, kv)


def delta_kernel(own_ref, rh_ref, rl_ref, state_ref, teacher_ref, delta_ref):
    for n in range(DSTEP):
        student = own_ref[n] + mm3(loaded((rh_ref, rl_ref), n), split(state_ref[n]), NT)
        delta = split(student - teacher_ref[:, HD * n : HD * (n + 1)].astype(f32))
        delta_ref[0, :, HD * n : HD * (n + 1)] = delta[0]
        delta_ref[1, :, HD * n : HD * (n + 1)] = delta[1]


def student_delta(half, own, reach, state, teacher):
    rows = pl.BlockSpec((DSTEP, HALF, HD), lambda h: (h, half, 0))
    return heads_call(
        delta_kernel, f"delta_{half}", 2,
        [rows, rows, rows, per_head(HD, HD, step=DSTEP), pl.BlockSpec((HALF, DSTEP * HD), lambda h: (0, h))],
        pl.BlockSpec((2, HALF, DSTEP * HD), lambda h: (0, 0, h)),
        jax.ShapeDtypeStruct((2, HALF, HEADS * HD), bf16),
        step=DSTEP,
    )(own, *reach, state, teacher)


def solve_back(refs_l, refs_d, n, right):
    solved, out = None, []
    for j in range(NB - 1, -1, -1):
        lo, hi = BLK * j, BLK * (j + 1)
        rest = right[j]
        if solved is not None:
            rest = rest - mm3(block_column(refs_l, n, j, j + 1), solved, TN)
        y = mm3((refs_d[0][n, lo:hi, :], refs_d[1][n, lo:hi, :]), split(rest), TN)
        out.append(y)
        solved = split(y) if solved is None else stack(split(y), solved)
    return solved, out[::-1]


def ready_kernel(
    xh_ref, xl_ref, lh_ref, ll_ref, dh_ref, dl_ref, ukh_ref, ukl_ref, cols_ref, state_ref, ah_ref, al_ref,
    nh_ref, nl_ref, th_ref, tl_ref, bh_ref, bl_ref,
):
    for n in range(STEP):
        found = [None] * NB
        for j in range(NB - 1, -1, -1):
            rest = block_column((ah_ref, al_ref), n, j, j)
            if j < NB - 1:
                rest = rest[0].astype(f32) + rest[1].astype(f32)
                for i in range(j + 1, NB):
                    more = mm3(found[i], block((lh_ref, ll_ref), n, i, j), NN)
                    at = BLK * (i - j)
                    rest = jnp.concatenate([rest[:at], rest[at:] - more], axis=0)
                rest = split(rest)
            d = dh_ref[n, BLK * j : BLK * (j + 1), :], dl_ref[n, BLK * j : BLK * (j + 1), :]
            found[j] = split(mm3(rest, d, NN))
            for i in range(j, NB):
                at, left = PACKED[i]
                for ref, part in zip((bh_ref, bl_ref), found[j]):
                    ref[n, at : at + BLK, left + BLK * j : left + BLK * (j + 1)] = part[BLK * (i - j) : BLK * (i - j + 1)]
        x = loaded((xh_ref, xl_ref), n)
        state = split(state_ref[n])
        first = x[0][:, :HD].astype(f32) + x[1][:, :HD].astype(f32)
        store((nh_ref, nl_ref), n, split(first - mm3((x[0][:, HD:], x[1][:, HD:]), state, NT)))
        uk = ukh_ref[n].astype(f32) + ukl_ref[n].astype(f32)
        moved = column_of(cols_ref, n, TAIL) * uk
        solved, _ = solve_back(
            (lh_ref, ll_ref), (dh_ref, dl_ref), n, [moved[BLK * j : BLK * (j + 1)] for j in range(NB)]
        )
        store((th_ref, tl_ref), n, solved)


def student_ready(solved, lower, inverse, uk, cols, state, attend):
    return heads_call(
        ready_kernel, "backward_ready", 10,
        [
            per_head(ROWS, 2 * HD), per_head(ROWS, 2 * HD), per_head(*TRI), per_head(*TRI),
            per_head(ROWS, BLK), per_head(ROWS, BLK), per_head(ROWS, HD), per_head(ROWS, HD),
            per_head(ROWS, 8), per_head(HD, HD), per_head(*TRI), per_head(*TRI),
        ],
        [per_head(ROWS, HD)] * 4 + [per_head(*TRI)] * 2,
        pair_shape(ROWS, HD) + pair_shape(ROWS, HD) + pair_shape(*TRI),
    )(*solved, *lower, *inverse, *uk, cols, state, *attend)


def project_kernel(core_ref, mine_ref, other_ref, w_mine_ref, w_other_ref, out_ref):
    width = HEADS * HD
    both = mm(mine_ref[...].reshape(2 * HALF, width), w_mine_ref[...], NN)
    both = both + mm(other_ref[...].reshape(2 * HALF, width), w_other_ref[...], NN)
    total = both[:HALF] + both[HALF:]
    largest = jnp.max(jnp.max(jnp.abs(total), axis=1, keepdims=True), axis=0, keepdims=True)
    exponent = exponent_of(largest)
    scaled = total * jnp.exp2(exponent)
    for p in range(PSTEP):
        at = slice(PIECE * p, PIECE * (p + 1))
        out_ref[p, :HALF, :] = scaled[:, at]
        out_ref[p, HALF:, :] = jnp.broadcast_to(exponent, (PAD, PIECE))


def project(half, core, mine, other, w_mine, w_other):
    width = HEADS * HD
    return pl.pallas_call(
        project_kernel,
        grid_spec=pltpu.PrefetchScalarGridSpec(
            num_scalar_prefetch=1,
            grid=(CHIPS // PSTEP,),
            in_specs=[
                pl.BlockSpec((2, HALF, width), lambda j, c: (0, 0, 0)),
                pl.BlockSpec((2, HALF, width), lambda j, c: (0, 0, 0)),
                pl.BlockSpec((width, PSTEP * PIECE), lambda j, c: (0, c[0] * (CHIPS // PSTEP) + j)),
                pl.BlockSpec((width, PSTEP * PIECE), lambda j, c: (0, j)),
            ],
            out_specs=pl.BlockSpec((PSTEP, HALF + PAD, PIECE), lambda j, c: (j, 0, 0)),
        ),
        out_shape=jax.ShapeDtypeStruct((CHIPS, HALF + PAD, PIECE), f32),
        compiler_params=params(PROJECT_MIB),
        cost_estimate=cost(7),
        name=f"difference_part_{half}",
    )(core, mine, other, w_mine, w_other)


def back_project_kernel(
    core_ref, high_ref, low_ref, w_mine_ref, w_other_ref, mine_ref, other_ref, square_ref
):
    rows = (slice(0, HALF), slice(HALF + PAD, ROWS + PAD))
    both = jnp.concatenate([ref[0, at, :] for ref in (high_ref, low_ref) for at in rows], axis=0)
    mine = mm(both, w_mine_ref[...], NT)
    other = mm(both, w_other_ref[...], NT)
    mine = mine[:ROWS] + mine[ROWS:]
    other = other[:ROWS] + other[ROWS:]
    values = both[:ROWS].astype(f32) + both[ROWS:].astype(f32)
    square = jnp.sum((values * values).reshape(ROWS // 8, 8, PIECE), axis=0)

    @pl.when(pl.program_id(0) == 0)
    def _():
        mine_ref[...] = mine
        other_ref[...] = other
        square_ref[...] = square

    @pl.when(pl.program_id(0) > 0)
    def _():
        mine_ref[...] += mine
        other_ref[...] += other
        square_ref[...] += square


def back_project(core, high, low, w_mine, w_other):
    width = HEADS * HD
    columns = pl.BlockSpec((1, ROWS + 2 * PAD, PIECE), lambda j, c: (j, 0, 0))
    return pl.pallas_call(
        back_project_kernel,
        grid_spec=pltpu.PrefetchScalarGridSpec(
            num_scalar_prefetch=1,
            grid=(CHIPS,),
            in_specs=[
                columns,
                columns,
                pl.BlockSpec((width, PIECE), lambda j, c: (0, c[0] * CHIPS + j)),
                pl.BlockSpec((width, PIECE), lambda j, c: (0, j)),
            ],
            out_specs=[
                pl.BlockSpec((ROWS, width), lambda j, c: (0, 0)),
                pl.BlockSpec((ROWS, width), lambda j, c: (0, 0)),
                pl.BlockSpec((8, PIECE), lambda j, c: (0, 0)),
            ],
        ),
        out_shape=[
            jax.ShapeDtypeStruct((ROWS, width), f32),
            jax.ShapeDtypeStruct((ROWS, width), f32),
            jax.ShapeDtypeStruct((8, PIECE), f32),
        ],
        compiler_params=params(BACK_MIB),
        cost_estimate=cost(14),
        name="head_grad_part",
    )(core, high, low, w_mine, w_other)


def state_grad_kernel(mine_ref, other_ref, rh_ref, rl_ref, gh_ref, gl_ref, out_ref):
    for n in range(DSTEP):
        at = slice(HD * n, HD * (n + 1))
        grad = split(mine_ref[:, at] + other_ref[:, at])
        gh_ref[:, at] = grad[0]
        gl_ref[:, at] = grad[1]
        out_ref[n] = mm3(grad, loaded((rh_ref, rl_ref), n), TN)


def state_grad_local(mine, other, reach):
    return heads_call(
        state_grad_kernel, "state_grad_local", 4,
        [columns_spec(DSTEP), columns_spec(DSTEP), per_head(ROWS, HD, step=DSTEP), per_head(ROWS, HD, step=DSTEP)],
        [columns_spec(DSTEP), columns_spec(DSTEP), per_head(HD, HD, step=DSTEP)],
        [jax.ShapeDtypeStruct((ROWS, HEADS * HD), bf16)] * 2
        + [jax.ShapeDtypeStruct((HEADS, HD, HD), f32)],
        step=DSTEP,
    )(mine, other, *reach)


def inner_kernel(gh_ref, gl_ref, bh_ref, bl_ref, y_ref):
    for n in range(DSTEP):
        at = slice(HD * n, HD * (n + 1))
        grad = gh_ref[:, at], gl_ref[:, at]
        for j in range(NB):
            lo, hi = BLK * j, BLK * (j + 1)
            y_ref[n, lo:hi, :] = mm3(block_column((bh_ref, bl_ref), n, j, j), rows_of(grad, lo, ROWS), TN)


def inner_grad(grad, through):
    return heads_call(
        inner_kernel, "update_grad_local", 4,
        [
            columns_spec(DSTEP), columns_spec(DSTEP),
            per_head(*TRI, step=DSTEP), per_head(*TRI, step=DSTEP),
        ],
        per_head(ROWS, HD, step=DSTEP),
        jax.ShapeDtypeStruct((HEADS, ROWS, HD), f32),
        step=DSTEP,
    )(*grad, *through)


def query_grad_kernel(
    gh_ref, gl_ref, nh_ref, nl_ref, row_ref, ukh_ref, ukl_ref, uqh_ref, uql_ref,
    cols_ref, inverse_ref, state_ref, q_ref, grad_ref, key_ref,
):
    for n in range(STEP):
        at = slice(HD * n, HD * (n + 1))
        grad = gh_ref[:, at], gl_ref[:, at]
        updates = loaded((nh_ref, nl_ref), n)
        uks, uqs = loaded((ukh_ref, ukl_ref), n), loaded((uqh_ref, uql_ref), n)
        from_state = column_of(cols_ref, n, GROWTH) * mm3(grad, split(state_ref[n]), NN)
        total = [None] * NB
        query_total = []
        for i in range(NB):
            lo, hi = BLK * i, BLK * (i + 1)
            outer = mm3(rows_of(grad, lo, hi), rows_of(updates, 0, hi), NT)
            through = split(outer * decays(column_of(cols_ref, n, COLUMN), row_ref[n], i))
            query_total.append(from_state[lo:hi] + mm3(through, rows_of(uks, 0, hi), NN))
            columns = mm3(through, rows_of(uqs, lo, hi), TN)
            for j in range(i + 1):
                more = columns[BLK * j : BLK * (j + 1)]
                total[j] = more if total[j] is None else total[j] + more
        for j in range(NB):
            key_ref[n, BLK * j : BLK * (j + 1), :] = total[j]
        uq = uqs[0].astype(f32) + uqs[1].astype(f32)
        query_grad = jnp.concatenate(query_total, axis=0)
        query_grad = split(through_unit(query_grad, uq, inverse_ref[n, :, :1]))
        q = q_ref[:, at]
        grad_ref[n] = halves(mm(q, beside(*query_grad), TN))


def query_grad_local(grad, updates, row, uk, uq, cols, inverse, state, queries):
    return heads_call(
        query_grad_kernel, "query_grad", 8,
        [
            columns_spec(), columns_spec(), per_head(ROWS, HD), per_head(ROWS, HD), per_head(1, ROWS),
            per_head(ROWS, HD), per_head(ROWS, HD), per_head(ROWS, HD), per_head(ROWS, HD),
            per_head(ROWS, 8), per_head(ROWS, 8), per_head(HD, HD), columns_spec(),
        ],
        [per_head(HD, HD), per_head(ROWS, HD)],
        [
            jax.ShapeDtypeStruct((HEADS, HD, HD), f32),
            jax.ShapeDtypeStruct((HEADS, ROWS, HD), f32),
        ],
    )(*grad, *updates, row, *uk, *uq, cols, inverse, state, queries)


def key_grad_kernel(
    y_ref, th_ref, tl_ref, nh_ref, nl_ref, row_ref, ukh_ref, ukl_ref,
    cols_ref, state_ref, state_grad_ref, key_ref, k_ref, grad_ref,
):
    for n in range(STEP):
        updates, uks = loaded((nh_ref, nl_ref), n), loaded((ukh_ref, ukl_ref), n)
        state_grad = split(state_grad_ref[n])
        inner = split(y_ref[n] + mm3(loaded((th_ref, tl_ref), n), state_grad, NT))
        write = column_of(cols_ref, n, WRITE)
        base = key_ref[n] + column_of(cols_ref, n, TAIL) * mm3(updates, state_grad, NN)
        base = base - column_of(cols_ref, n, WRITE_GROWTH) * mm3(inner, split(state_ref[n]), NN)
        total = [base[BLK * j : BLK * (j + 1)] for j in range(NB)]
        for i in range(NB):
            lo, hi = BLK * i, BLK * (i + 1)
            outer = mm3(rows_of(inner, lo, hi), rows_of(updates, 0, hi), NT)
            scaled = outer * decays(column_of(cols_ref, n, COLUMN), row_ref[n], i) * write[lo:hi]
            through = split(jnp.where(strict(i), scaled, 0.0))
            total[i] = total[i] - mm3(through, rows_of(uks, 0, hi), NN)
            columns = mm3(through, rows_of(uks, lo, hi), TN)
            for j in range(i + 1):
                total[j] = total[j] - columns[BLK * j : BLK * (j + 1)]
        uk = uks[0].astype(f32) + uks[1].astype(f32)
        key_grad = jnp.concatenate(total, axis=0)
        key_grad = split(through_unit(key_grad, uk, column_of(cols_ref, n, INVERSE)))
        grad_ref[n] = halves(mm(k_ref[...], beside(*key_grad), TN))


def key_grad_local(inner, moved, updates, row, uk, cols, state, state_grad, partial, key_mine):
    return heads_call(
        key_grad_kernel, "key_grad", 9,
        [
            per_head(ROWS, HD), per_head(ROWS, HD), per_head(ROWS, HD), per_head(ROWS, HD),
            per_head(ROWS, HD), per_head(1, ROWS), per_head(ROWS, HD), per_head(ROWS, HD),
            per_head(ROWS, 8), per_head(HD, HD), per_head(HD, HD), per_head(ROWS, HD), whole(ROWS, HD),
        ],
        per_head(HD, HD),
        jax.ShapeDtypeStruct((HEADS, HD, HD), f32),
    )(inner, *moved, *updates, row, *uk, cols, state, state_grad, partial, key_mine)


def exponent_of(largest):
    return jnp.clip(14.0 - jnp.ceil(jnp.log2(jnp.maximum(largest, 1e-30))), -100.0, 100.0)


def summed(pieces):
    exponents = pieces[:, -1:, :].astype(f32)
    exponent = jnp.min(exponents, axis=0) - 3.0
    total = jnp.sum(pieces.astype(f32) * jnp.exp2(exponent[None] - exponents), axis=0)
    at = lax.broadcasted_iota(jnp.int32, total.shape, 0)
    return jnp.where(at < total.shape[0] - PAD, total, exponent).astype(f16)


def rescaled(message):
    return message.astype(f32) * jnp.exp2(-message[..., -1:, :].astype(f32))


def transpose_over(x, axis, groups=None):
    return lax.all_to_all(x, axis, 0, 0, axis_index_groups=groups, tiled=True)


def shards(queries, key_heads, values, log_decay, write_strength, query_map, key_map, out_weight):
    ctx = lax.axis_index("ctx")
    head_index = lax.axis_index("head")
    core = lax.rem(head_index, 2)
    kv_column = head_index * HEADS // (QUERY_HEAD_COUNT // KVH) * HD
    key_mine = lax.dynamic_slice_in_dim(key_heads, kv_column, HD, 1)
    value_mine = lax.dynamic_slice_in_dim(values, kv_column, HD, 1)
    kv = lax.all_gather(
        jnp.concatenate([key_mine, value_mine], axis=1), "ctx", axis=0, tiled=True
    )
    cols, row, *pairs, message = student_keys(
        key_mine, value_mine, log_decay, write_strength, key_map
    )
    uk, lower, inverse, solved = [pairs[2 * i : 2 * i + 2] for i in range(4)]
    ctx_scalar = ctx.astype(jnp.int32).reshape(1)
    core_scalar = core.astype(jnp.int32).reshape(1)
    messages = transpose_over(message, "ctx")
    partner = [(i, i ^ 1) for i in range(2 * CHIPS)]
    half = D // 2
    core_after, _ = lax.optimization_barrier((core, message))
    w_other = lax.ppermute(
        lax.dynamic_slice_in_dim(out_weight, (1 - core_after) * half, half, 1), "head", partner
    )
    cols_after, _ = lax.optimization_barrier((cols, message))
    q_inverse, *pairs = student_queries(queries, query_map, cols_after, row, uk, solved)
    uq, attend, own, reach = pairs[:2], pairs[2:4], pairs[4], pairs[5:]
    messages, own = lax.optimization_barrier((messages, own))
    states = chain(messages)
    state = transpose_over(states, "ctx").reshape(HEADS, HD, HD)
    kv, ctx_scalar, _ = lax.optimization_barrier((kv, ctx_scalar, states))
    sent, message_out = [], states
    for half in range(2):
        kv, ctx_scalar, _ = lax.optimization_barrier((kv, ctx_scalar, message_out))
        teacher = teacher_out(half, ctx_scalar, queries, kv)
        state_here, teacher = lax.optimization_barrier((state, teacher))
        delta = student_delta(half, own, reach, state_here, teacher)
        delta_other = lax.ppermute(delta, "head", partner)
        part = project(half, core_scalar, delta, delta_other, out_weight, w_other)
        message_out = part.astype(f16)
        sent.append(transpose_over(message_out, "head", SAME_CORE))
    state_after, _ = lax.optimization_barrier((state, message_out))
    *pairs, = student_ready(solved, lower, inverse, uk, cols, state_after, attend)
    sent[1], pairs = lax.optimization_barrier((sent[1], pairs))
    updates, moved, through = pairs[:2], pairs[2:4], pairs[4:]
    gathered = lax.all_gather(
        jnp.concatenate([summed(pieces) for pieces in sent], axis=0),
        "head", axis=0, axis_index_groups=SAME_CORE, tiled=False,
    )
    columns_high, columns_low = split(rescaled(gathered.reshape(CHIPS, 2, HALF + PAD, PIECE)))
    together = (CHIPS, ROWS + 2 * PAD, PIECE)
    grad_mine, grad_other, squares = back_project(
        core_scalar, columns_high.reshape(together), columns_low.reshape(together), out_weight, w_other
    )
    square_mine = jnp.broadcast_to(jnp.sum(squares), (8, HD))
    square_other = lax.ppermute(square_mine, "head", partner)
    grad_high, grad_low, local = state_grad_local(
        grad_mine, lax.ppermute(grad_other, "head", partner), reach
    )
    locals_ = transpose_over(local.reshape(CTX, HD // 2, HD), "ctx")
    (grad_high, grad_low), _ = lax.optimization_barrier(((grad_high, grad_low), local))
    head_grad = [grad_high, grad_low]
    query_grad, partial = query_grad_local(
        head_grad, updates, row, uk, uq, cols, q_inverse, state, queries
    )
    locals_, partial = lax.optimization_barrier((locals_, partial))
    states_back = back_chain(messages, locals_)
    state_grad = transpose_over(states_back, "ctx").reshape(HEADS, HD, HD)
    through_after, _ = lax.optimization_barrier((through, states_back))
    inner = inner_grad(head_grad, through_after)
    key_grad = key_grad_local(
        inner, moved, updates, row, uk, cols, state, state_grad, partial, key_mine
    )
    grads = jnp.concatenate([query_grad, key_grad], axis=0)
    extra = jnp.broadcast_to(square_mine + square_other, (2 * HEADS, 8, HD))
    shared = transpose_over(jnp.concatenate([grads, extra], axis=1), "ctx")
    total = jnp.sum(shared, axis=0, keepdims=True)
    final = transpose_over(jnp.broadcast_to(total, (CTX,) + total.shape[1:]), "ctx")
    normalizer = CTX * ROWS * D
    return final[0, HD, 0] / normalizer, final[:HEADS, :HD], final[HEADS:, :HD]


def solution(mesh):
    placed = (
        P("ctx", "head"),
        P("ctx", None),
        P("ctx", None),
        P("ctx", "head"),
        P("ctx", "head"),
        P("head", None, None),
        P("head", None, None),
        P("head", None),
    )
    return jax.shard_map(
        shards,
        mesh=mesh,
        in_specs=placed,
        out_specs=(P(), P("head", None, None), P("head", None, None)),
        check_vma=False,
    )
```

```python
import functools
import math

import jax
import jax.numpy as jnp
from jax import lax
from jax.experimental import pallas as pl
from jax.experimental.pallas import tpu as pltpu
from jax.sharding import PartitionSpec as P

D = 8192
QUERY_HEAD_COUNT = 64
KVH = 8
HD = 128
ROWS = 512
BLK = 128
NB = ROWS // BLK
TRI = (2 * BLK, 5 * BLK)
HEADS = 4
CTX = 8
CHIPS = 8
PIECE = 512
PAD = 8
SAME_CORE = [[2 * p + core for p in range(CHIPS)] for core in range(2)]

f32 = jnp.float32
bf16 = jnp.bfloat16
f16 = jnp.float16

MIB = 1024 * 1024
FLOOR = 0
PROJECT_MIB = 45
BACK_MIB = 44
PSTEP = 2
STEP = 1
HALF = ROWS // 2
KSTEP = 4
DSTEP = 2
TEACH = 4


def params(mib):
    return pltpu.CompilerParams(vmem_limit_bytes=max(mib, FLOOR) * MIB)


def cost(micros):
    return pl.CostEstimate(flops=int(micros * 1.1e9), bytes_accessed=0, transcendentals=0)


def split(x):
    high = x.astype(bf16)
    return high, (x - high.astype(f32)).astype(bf16)


NN = (((1,), (0,)), ((), ()))
NT = (((1,), (1,)), ((), ()))
TN = (((0,), (0,)), ((), ()))


def mm(a, b, dims):
    return lax.dot_general(a, b, dims, preferred_element_type=f32)


def beside(a, b):
    return jnp.concatenate([a, b], axis=1)


def above(a, b):
    return jnp.concatenate([a, b], axis=0)


def halves(x):
    n = x.shape[1] // 2
    return x[:, :n] + x[:, n:]


def mm3(a, b, dims):
    depth_at = dims[0][0][0]
    depth = a[0].shape[depth_at]
    if depth <= 128:
        left = beside(*a) if depth_at == 1 else above(*a)
        if dims is NT:
            return halves(mm(left, above(beside(b[0], b[0]), beside(b[1], b[1])), dims))
        if b[0].shape[1] <= 128:
            wide = beside(*b)
            return halves(mm(left, above(wide, wide), dims))
        return mm(left, above(b[0], b[0]), dims) + mm(a[0], b[1], dims)
    if dims is not NT and b[0].shape[1] <= 128:
        return halves(mm(a[0], beside(*b), dims)) + mm(a[1], b[0], dims)
    return mm(a[0], b[0], dims) + (mm(a[0], b[1], dims) + mm(a[1], b[0], dims))


def rows_of(pair, lo, hi):
    return pair[0][lo:hi], pair[1][lo:hi]


def stack(a, b):
    return above(a[0], b[0]), above(a[1], b[1])


PACKED = ((0, 4 * BLK), (BLK, 3 * BLK), (BLK, 0), (0, 0))


def block(refs, n, i, j):
    at, left = PACKED[i]
    return tuple(ref[n, at : at + BLK, left + BLK * j : left + BLK * (j + 1)] for ref in refs)


def block_column(refs, n, j, first):
    parts = []
    for ref in refs:
        blocks = []
        for i in range(first, NB):
            at, left = PACKED[i]
            blocks.append(ref[n, at : at + BLK, left + BLK * j : left + BLK * (j + 1)])
        parts.append(jnp.concatenate(blocks, axis=0))
    return tuple(parts)


def store_row(refs, n, i, pair):
    at, left = PACKED[i]
    for ref, part in zip(refs, pair):
        ref[n, at : at + BLK, left : left + BLK * (i + 1)] = part


def joined(blocks):
    return tuple(
        jnp.concatenate([jnp.concatenate([b[p] for b in line], axis=1) for line in blocks], axis=0)
        for p in range(2)
    )


def loaded(refs, n):
    return refs[0][n], refs[1][n]


def store(refs, n, pair):
    refs[0][n] = pair[0]
    refs[1][n] = pair[1]


def unit(x):
    inverse = 1.0 / jnp.sqrt(jnp.sum(x * x, axis=-1, keepdims=True) + 1e-06)
    return x * inverse, inverse


def through_unit(grad, units, inverse):
    return inverse * (grad - units * jnp.sum(units * grad, axis=1, keepdims=True))


def gate_forms(gate_row, write_row):
    ii = lax.broadcasted_iota(jnp.int32, (ROWS, ROWS), 0)
    jj = lax.broadcasted_iota(jnp.int32, (ROWS, ROWS), 1)
    gate = jnp.sum(jnp.where(ii == jj, gate_row, 0.0), axis=1, keepdims=True)
    write = jnp.sum(jnp.where(ii == jj, write_row, 0.0), axis=1, keepdims=True)
    column = jnp.sum(jnp.where(jj <= ii, gate_row, 0.0), axis=1, keepdims=True)
    row = jnp.sum(jnp.where(ii <= jj, gate, 0.0), axis=0, keepdims=True)
    return column, row, write


def decays(column, row, i):
    width = BLK * (i + 1)
    ii = lax.broadcasted_iota(jnp.int32, (BLK, width), 0) + BLK * i
    jj = lax.broadcasted_iota(jnp.int32, (BLK, width), 1)
    inclusive = ii >= jj
    gap = column[BLK * i : width] - row[:, :width]
    return jnp.where(inclusive, jnp.exp(jnp.where(inclusive, gap, 0.0)), 0.0)


def strict(i):
    width = BLK * (i + 1)
    ii = lax.broadcasted_iota(jnp.int32, (BLK, width), 0) + BLK * i
    return ii > lax.broadcasted_iota(jnp.int32, (BLK, width), 1)


def inverses(blocks):
    ii = lax.broadcasted_iota(jnp.int32, (BLK, BLK), 0)
    jj = lax.broadcasted_iota(jnp.int32, (BLK, BLK), 1)
    diagonal = (ii == jj).astype(f32)
    first = ((ii >> 1) == (jj >> 1)) & (ii > jj)
    found = [split(diagonal - jnp.where(first, block, 0.0)) for block in blocks]
    whole_parts = [split(-block) for block in blocks]
    none = jnp.zeros((BLK, BLK), bf16)
    shift = 1
    while (1 << shift) < BLK:
        mask = ((ii >> (shift + 1)) == (jj >> (shift + 1))) & ((ii >> shift) > (jj >> shift))
        corner = [tuple(jnp.where(mask, part, none) for part in pair) for pair in whole_parts]
        inner = [split(mm3(c, x, NN)) for c, x in zip(corner, found)]
        more = [split(mm3(x, y, NN)) for x, y in zip(found, inner)]
        found = [(x[0] + y[0], x[1] + y[1]) for x, y in zip(found, more)]
        shift += 1
    return found


GROWTH, TAIL, WRITE, WRITE_GROWTH, INVERSE, COLUMN = range(6)


def column_of(ref, n, which):
    return ref[n, :, which : which + 1]


def per_head(*shape, step=None):
    return pl.BlockSpec((step or STEP,) + shape, lambda h, *_: (h,) + (0,) * len(shape))


def whole(*shape):
    return pl.BlockSpec(shape, lambda h, *_: (0,) * len(shape))


def columns_spec(step=None):
    return pl.BlockSpec((ROWS, (step or STEP) * HD), lambda h, *_: (0, h))


def pair_shape(*shape):
    return [jax.ShapeDtypeStruct((HEADS,) + shape, bf16)] * 2


def heads_call(kernel, name, micros, in_specs, out_specs, out_shape, mib=56, step=None):
    return pl.pallas_call(
        kernel,
        grid=(HEADS // (step or STEP),),
        in_specs=in_specs,
        out_specs=out_specs,
        out_shape=out_shape,
        compiler_params=params(mib),
        cost_estimate=cost(micros),
        name=name,
    )


def keys_kernel(
    k_ref, v_ref, gate_ref, write_ref, kmap_ref,
    cols_ref, row_ref, ukh_ref, ukl_ref, lh_ref, ll_ref, dh_ref, dl_ref, xh_ref, xl_ref, message_ref,
):
    heads = range(KSTEP)
    lower, uks, columns, rights, ends = [], [], [], [], []
    for n in heads:
        column, row, write = gate_forms(
            gate_ref[pl.ds(pl.program_id(0) * KSTEP + n, 1), :],
            write_ref[pl.ds(pl.program_id(0) * KSTEP + n, 1), :],
        )
        end = row[:, ROWS - 1 : ROWS]
        growth = jnp.exp(column)
        tail = jnp.exp(end - column)
        uk, inverse = unit(mm(k_ref[...], kmap_ref[n], NN))
        pair = split(uk)
        store((ukh_ref, ukl_ref), n, pair)
        for which, value in enumerate((growth, tail, write, write * growth, inverse, column)):
            cols_ref[n, :, which : which + 1] = value
        row_ref[n] = row
        own = []
        for i in range(NB):
            lo, hi = BLK * i, BLK * (i + 1)
            gram = mm3(rows_of(pair, lo, hi), rows_of(pair, 0, hi), NT)
            decay = decays(column, row, i)
            own.append(jnp.where(strict(i), gram * decay * write[lo:hi], 0.0))
        lower.append(own)
        uks.append(split(tail * uk))
        rights.append(beside(write * v_ref[...].astype(f32), (write * growth) * uk))
        ends.append(end)
    found = inverses([lower[n][i][:, BLK * i :] for n in heads for i in range(NB)])
    inverse = [[found[n * NB + i] for i in range(NB)] for n in heads]
    solved = [None] * KSTEP
    for i in range(NB):
        lo, hi = BLK * i, BLK * (i + 1)
        for n in heads:
            low = split(lower[n][i])
            store_row((lh_ref, ll_ref), n, i, low)
            dh_ref[n, lo:hi, :] = inverse[n][i][0]
            dl_ref[n, lo:hi, :] = inverse[n][i][1]
            rest = rights[n][lo:hi]
            if i:
                rest = rest - mm3((low[0][:, :lo], low[1][:, :lo]), solved[n], NN)
            x = split(mm3(inverse[n][i], split(rest), NN))
            solved[n] = stack(solved[n], x) if i else x
    ii = lax.broadcasted_iota(jnp.int32, (HD, HD), 0)
    jj = lax.broadcasted_iota(jnp.int32, (HD, HD), 1)
    half = HD // 2
    for n in heads:
        store((xh_ref, xl_ref), n, solved[n])
        moved = mm3(solved[n], uks[n], TN)
        carry = jnp.where(ii == jj, jnp.exp(ends[n]), 0.0) - moved[HD:]
        for s in range(2):
            message_ref[2 * n + s, :half, :] = moved[half * s : half * (s + 1)]
            message_ref[2 * n + s, half:, :] = carry


def student_keys(key_mine, value_mine, log_decay, write_strength, key_map):
    return heads_call(
        keys_kernel, "student_keys", 16,
        [whole(ROWS, HD), whole(ROWS, HD), whole(HEADS, ROWS), whole(HEADS, ROWS), per_head(HD, HD, step=KSTEP)],
        [
            per_head(ROWS, 8, step=KSTEP), per_head(1, ROWS, step=KSTEP),
            per_head(ROWS, HD, step=KSTEP), per_head(ROWS, HD, step=KSTEP),
            per_head(*TRI, step=KSTEP), per_head(*TRI, step=KSTEP),
            per_head(ROWS, BLK, step=KSTEP), per_head(ROWS, BLK, step=KSTEP),
            per_head(ROWS, 2 * HD, step=KSTEP), per_head(ROWS, 2 * HD, step=KSTEP),
            pl.BlockSpec((2 * KSTEP, HD + HD // 2, HD), lambda h: (h, 0, 0)),
        ],
        [
            jax.ShapeDtypeStruct((HEADS, ROWS, 8), f32),
            jax.ShapeDtypeStruct((HEADS, 1, ROWS), f32),
            *pair_shape(ROWS, HD), *pair_shape(*TRI), *pair_shape(ROWS, BLK), *pair_shape(ROWS, 2 * HD),
            jax.ShapeDtypeStruct((2 * HEADS, HD + HD // 2, HD), f32),
        ],
        step=KSTEP,
    )(key_mine, value_mine, log_decay.T, write_strength.T, key_map)


def queries_kernel(
    q_ref, qmap_ref, cols_ref, row_ref, ukh_ref, ukl_ref, xh_ref, xl_ref,
    inverse_ref, uqh_ref, uql_ref, ah_ref, al_ref, own_ref, rh_ref, rl_ref,
):
    for n in range(STEP):
        uq, inverse = unit(mm(q_ref[:, HD * n : HD * (n + 1)], qmap_ref[n], NN))
        inverse_ref[n, :, :1] = inverse
        uqs = split(uq)
        store((uqh_ref, uql_ref), n, uqs)
        uks = loaded((ukh_ref, ukl_ref), n)
        solved = loaded((xh_ref, xl_ref), n)
        reach = column_of(cols_ref, n, GROWTH) * uq
        for i in range(NB):
            lo, hi = BLK * i, BLK * (i + 1)
            decay = decays(column_of(cols_ref, n, COLUMN), row_ref[n], i)
            attend = split(mm3(rows_of(uqs, lo, hi), rows_of(uks, 0, hi), NT) * decay)
            store_row((ah_ref, al_ref), n, i, attend)
            z = mm3(attend, rows_of(solved, 0, hi), NN)
            own_ref[n, lo:hi, :] = z[:, :HD]
            part = split(reach[lo:hi] - z[:, HD:])
            rh_ref[n, lo:hi, :] = part[0]
            rl_ref[n, lo:hi, :] = part[1]


def student_queries(queries, query_map, cols, row, uk, solved):
    return heads_call(
        queries_kernel, "student_queries", 8,
        [
            columns_spec(), per_head(HD, HD), per_head(ROWS, 8), per_head(1, ROWS),
            per_head(ROWS, HD), per_head(ROWS, HD), per_head(ROWS, 2 * HD), per_head(ROWS, 2 * HD),
        ],
        [
            per_head(ROWS, 8), per_head(ROWS, HD), per_head(ROWS, HD), per_head(*TRI),
            per_head(*TRI), per_head(ROWS, HD), per_head(ROWS, HD), per_head(ROWS, HD),
        ],
        [
            jax.ShapeDtypeStruct((HEADS, ROWS, 8), f32),
            *pair_shape(ROWS, HD), *pair_shape(*TRI),
            jax.ShapeDtypeStruct((HEADS, ROWS, HD), f32),
            *pair_shape(ROWS, HD),
        ],
    )(queries, query_map, cols, row, *uk, *solved)


def chain_kernel(message_ref, out_ref):
    half = HD // 2
    carries = [split(message_ref[c, half:, :]) for c in range(CTX - 1)]
    state = jnp.zeros((half, HD), f32)
    out_ref[0] = state
    for c in range(CTX - 1):
        state = mm3(split(state), carries[c], NN) + message_ref[c, :half, :]
        out_ref[c + 1] = state


def chain(messages):
    return pl.pallas_call(
        chain_kernel,
        out_shape=jax.ShapeDtypeStruct((CTX, HD // 2, HD), f32),
        compiler_params=params(8),
        cost_estimate=cost(3),
        name="state_chain",
    )(messages)


def back_chain_kernel(message_ref, grad_ref, out_ref):
    half = HD // 2
    carries = [split(message_ref[c, half:, :]) for c in range(CTX)]
    state = jnp.zeros((half, HD), f32)
    out_ref[CTX - 1] = state
    for c in range(CTX - 1, 0, -1):
        state = mm3(split(state), carries[c], NT) + grad_ref[c]
        out_ref[c - 1] = state


def back_chain(messages, grads):
    return pl.pallas_call(
        back_chain_kernel,
        out_shape=jax.ShapeDtypeStruct((CTX, HD // 2, HD), f32),
        compiler_params=params(8),
        cost_estimate=cost(3),
        name="state_grad_chain",
    )(messages, grads)


def teacher_kernel(half, ctx_ref, q_ref, kv_ref, out_ref):
    mine = ctx_ref[0]
    scale = math.log2(math.e) / math.sqrt(HD)

    def block(j, carry, width, diagonal):
        start = pl.multiple_of(j * ROWS, ROWS)
        keys = kv_ref[pl.ds(start, width), :HD]
        values = kv_ref[pl.ds(start, width), HD:]
        out = []
        raw = [mm(q_ref[:, HD * n : HD * (n + 1)], keys, NT) for n in range(TEACH)]
        for n in range(TEACH):
            top, total, mixed = carry[n]
            scores = raw[n]
            if diagonal:
                ii = lax.broadcasted_iota(jnp.int32, (HALF, width), 0) + HALF * half
                jj = lax.broadcasted_iota(jnp.int32, (HALF, width), 1)
                scores = jnp.where(jj <= ii, scores, -jnp.inf)
            new_top = jnp.maximum(top, jnp.max(scores, axis=1, keepdims=True))
            fade = jnp.exp2((top - new_top) * scale)
            weights = jnp.exp2((scores - new_top) * scale)
            total = total * fade + jnp.sum(weights, axis=1, keepdims=True)
            mixed = mixed * fade + mm(weights.astype(bf16), values, NN)
            out.append((new_top, total, mixed))
        return tuple(out)

    start = (
        jnp.full((HALF, 1), -jnp.inf, f32),
        jnp.zeros((HALF, 1), f32),
        jnp.zeros((HALF, HD), f32),
    )
    carry = block(mine, (start,) * TEACH, HALF * (half + 1), True)
    carry = lax.fori_loop(0, mine, lambda j, c: block(j, c, ROWS, False), carry)
    for n in range(TEACH):
        _, total, mixed = carry[n]
        out_ref[:, HD * n : HD * (n + 1)] = (mixed / total).astype(bf16)


def teacher_out(half, ctx, queries, kv):
    return pl.pallas_call(
        functools.partial(teacher_kernel, half),
        grid_spec=pltpu.PrefetchScalarGridSpec(
            num_scalar_prefetch=1,
            grid=(HEADS // TEACH,),
            in_specs=[
                pl.BlockSpec((HALF, TEACH * HD), lambda h, c: (half, h)),
                pl.BlockSpec((CTX * ROWS, 2 * HD), lambda h, c: (0, 0)),
            ],
            out_specs=pl.BlockSpec((HALF, TEACH * HD), lambda h, c: (0, h)),
        ),
        out_shape=jax.ShapeDtypeStruct((HALF, HEADS * HD), bf16),
        compiler_params=params(24),
        cost_estimate=cost(9),
        name=f"teacher_{half}",
    )(ctx, queries, kv)


def delta_kernel(own_ref, rh_ref, rl_ref, state_ref, teacher_ref, delta_ref):
    for n in range(DSTEP):
        student = own_ref[n] + mm3(loaded((rh_ref, rl_ref), n), split(state_ref[n]), NT)
        delta = split(student - teacher_ref[:, HD * n : HD * (n + 1)].astype(f32))
        delta_ref[0, :, HD * n : HD * (n + 1)] = delta[0]
        delta_ref[1, :, HD * n : HD * (n + 1)] = delta[1]


def student_delta(half, own, reach, state, teacher):
    rows = pl.BlockSpec((DSTEP, HALF, HD), lambda h: (h, half, 0))
    return heads_call(
        delta_kernel, f"delta_{half}", 2,
        [rows, rows, rows, per_head(HD, HD, step=DSTEP), pl.BlockSpec((HALF, DSTEP * HD), lambda h: (0, h))],
        pl.BlockSpec((2, HALF, DSTEP * HD), lambda h: (0, 0, h)),
        jax.ShapeDtypeStruct((2, HALF, HEADS * HD), bf16),
        mib=24,
        step=DSTEP,
    )(own, *reach, state, teacher)


def solve_back(refs_l, refs_d, n, right):
    solved, out = None, []
    for j in range(NB - 1, -1, -1):
        lo, hi = BLK * j, BLK * (j + 1)
        rest = right[j]
        if solved is not None:
            rest = rest - mm3(block_column(refs_l, n, j, j + 1), solved, TN)
        y = mm3((refs_d[0][n, lo:hi, :], refs_d[1][n, lo:hi, :]), split(rest), TN)
        out.append(y)
        solved = split(y) if solved is None else stack(split(y), solved)
    return solved, out[::-1]


def ready_kernel(
    xh_ref, xl_ref, lh_ref, ll_ref, dh_ref, dl_ref, ukh_ref, ukl_ref, cols_ref, state_ref, ah_ref, al_ref,
    nh_ref, nl_ref, th_ref, tl_ref, bh_ref, bl_ref,
):
    for n in range(STEP):
        found = [None] * NB
        for j in range(NB - 1, -1, -1):
            rest = block_column((ah_ref, al_ref), n, j, j)
            if j < NB - 1:
                rest = rest[0].astype(f32) + rest[1].astype(f32)
                for i in range(j + 1, NB):
                    more = mm3(found[i], block((lh_ref, ll_ref), n, i, j), NN)
                    at = BLK * (i - j)
                    rest = jnp.concatenate([rest[:at], rest[at:] - more], axis=0)
                rest = split(rest)
            d = dh_ref[n, BLK * j : BLK * (j + 1), :], dl_ref[n, BLK * j : BLK * (j + 1), :]
            found[j] = split(mm3(rest, d, NN))
            for i in range(j, NB):
                at, left = PACKED[i]
                for ref, part in zip((bh_ref, bl_ref), found[j]):
                    ref[n, at : at + BLK, left + BLK * j : left + BLK * (j + 1)] = part[BLK * (i - j) : BLK * (i - j + 1)]
        x = loaded((xh_ref, xl_ref), n)
        state = split(state_ref[n])
        first = x[0][:, :HD].astype(f32) + x[1][:, :HD].astype(f32)
        store((nh_ref, nl_ref), n, split(first - mm3((x[0][:, HD:], x[1][:, HD:]), state, NT)))
        uk = ukh_ref[n].astype(f32) + ukl_ref[n].astype(f32)
        moved = column_of(cols_ref, n, TAIL) * uk
        solved, _ = solve_back(
            (lh_ref, ll_ref), (dh_ref, dl_ref), n, [moved[BLK * j : BLK * (j + 1)] for j in range(NB)]
        )
        store((th_ref, tl_ref), n, solved)


def student_ready(solved, lower, inverse, uk, cols, state, attend):
    return heads_call(
        ready_kernel, "backward_ready", 10,
        [
            per_head(ROWS, 2 * HD), per_head(ROWS, 2 * HD), per_head(*TRI), per_head(*TRI),
            per_head(ROWS, BLK), per_head(ROWS, BLK), per_head(ROWS, HD), per_head(ROWS, HD),
            per_head(ROWS, 8), per_head(HD, HD), per_head(*TRI), per_head(*TRI),
        ],
        [per_head(ROWS, HD)] * 4 + [per_head(*TRI)] * 2,
        pair_shape(ROWS, HD) + pair_shape(ROWS, HD) + pair_shape(*TRI),
    )(*solved, *lower, *inverse, *uk, cols, state, *attend)


def project_kernel(core_ref, mine_ref, other_ref, w_mine_ref, w_other_ref, out_ref):
    width = HEADS * HD
    both = mm(mine_ref[...].reshape(2 * HALF, width), w_mine_ref[...], NN)
    both = both + mm(other_ref[...].reshape(2 * HALF, width), w_other_ref[...], NN)
    total = both[:HALF] + both[HALF:]
    largest = jnp.max(jnp.max(jnp.abs(total), axis=1, keepdims=True), axis=0, keepdims=True)
    exponent = exponent_of(largest)
    scaled = total * jnp.exp2(exponent)
    for p in range(PSTEP):
        at = slice(PIECE * p, PIECE * (p + 1))
        out_ref[p, :HALF, :] = scaled[:, at]
        out_ref[p, HALF:, :] = jnp.broadcast_to(exponent, (PAD, PIECE))


def project(half, core, mine, other, w_mine, w_other):
    width = HEADS * HD
    return pl.pallas_call(
        project_kernel,
        grid_spec=pltpu.PrefetchScalarGridSpec(
            num_scalar_prefetch=1,
            grid=(CHIPS // PSTEP,),
            in_specs=[
                pl.BlockSpec((2, HALF, width), lambda j, c: (0, 0, 0)),
                pl.BlockSpec((2, HALF, width), lambda j, c: (0, 0, 0)),
                pl.BlockSpec((width, PSTEP * PIECE), lambda j, c: (0, c[0] * (CHIPS // PSTEP) + j)),
                pl.BlockSpec((width, PSTEP * PIECE), lambda j, c: (0, c[0] * (CHIPS // PSTEP) + j)),
            ],
            out_specs=pl.BlockSpec((PSTEP, HALF + PAD, PIECE), lambda j, c: (j, 0, 0)),
        ),
        out_shape=jax.ShapeDtypeStruct((CHIPS, HALF + PAD, PIECE), f32),
        compiler_params=params(PROJECT_MIB),
        cost_estimate=cost(7),
        name=f"difference_part_{half}",
    )(core, mine, other, w_mine, w_other)


def back_project_kernel(
    core_ref, high_ref, low_ref, w_mine_ref, w_other_ref, mine_ref, other_ref, square_ref
):
    both = jnp.concatenate([high_ref[0, :ROWS, :], low_ref[0, :ROWS, :]], axis=0)
    mine = mm(both, w_mine_ref[...], NT)
    other = mm(both, w_other_ref[...], NT)
    mine = mine[:ROWS] + mine[ROWS:]
    other = other[:ROWS] + other[ROWS:]
    values = both[:ROWS].astype(f32) + both[ROWS:].astype(f32)
    square = jnp.sum((values * values).reshape(ROWS // 8, 8, PIECE), axis=0)

    @pl.when(pl.program_id(0) == 0)
    def _():
        mine_ref[...] = mine
        other_ref[:ROWS, :] = other
        other_ref[ROWS:, :] = square
        square_ref[...] = square

    @pl.when(pl.program_id(0) > 0)
    def _():
        mine_ref[...] += mine
        other_ref[:ROWS, :] += other
        other_ref[ROWS:, :] += square
        square_ref[...] += square


def back_project(core, high, low, w_mine, w_other):
    width = HEADS * HD
    columns = pl.BlockSpec((1, ROWS + 2 * PAD, PIECE), lambda j, c: (j, 0, 0))
    return pl.pallas_call(
        back_project_kernel,
        grid_spec=pltpu.PrefetchScalarGridSpec(
            num_scalar_prefetch=1,
            grid=(CHIPS,),
            in_specs=[
                columns,
                columns,
                pl.BlockSpec((width, PIECE), lambda j, c: (0, c[0] * CHIPS + j)),
                pl.BlockSpec((width, PIECE), lambda j, c: (0, c[0] * CHIPS + j)),
            ],
            out_specs=[
                pl.BlockSpec((ROWS, width), lambda j, c: (0, 0)),
                pl.BlockSpec((ROWS + 8, width), lambda j, c: (0, 0)),
                pl.BlockSpec((8, PIECE), lambda j, c: (0, 0)),
            ],
        ),
        out_shape=[
            jax.ShapeDtypeStruct((ROWS, width), f32),
            jax.ShapeDtypeStruct((ROWS + 8, width), f32),
            jax.ShapeDtypeStruct((8, PIECE), f32),
        ],
        compiler_params=params(BACK_MIB),
        cost_estimate=cost(14),
        name="head_grad_part",
    )(core, high, low, w_mine, w_other)


def state_grad_kernel(
    mine_ref, other_ref, square_ref, rh_ref, rl_ref, gh_ref, gl_ref, out_ref, total_ref
):
    for n in range(DSTEP):
        at = slice(HD * n, HD * (n + 1))
        grad = split(mine_ref[:, at] + other_ref[:ROWS, at])
        gh_ref[:, at] = grad[0]
        gl_ref[:, at] = grad[1]
        out_ref[n] = mm3(grad, loaded((rh_ref, rl_ref), n), TN)
        total_ref[n] = square_ref[:, at] + other_ref[ROWS:, at]


def state_grad_local(mine, other, squares, reach):
    return heads_call(
        state_grad_kernel, "state_grad_local", 2,
        [
            columns_spec(DSTEP),
            pl.BlockSpec((ROWS + 8, DSTEP * HD), lambda h: (0, h)),
            pl.BlockSpec((8, DSTEP * HD), lambda h: (0, h)),
            per_head(ROWS, HD, step=DSTEP), per_head(ROWS, HD, step=DSTEP),
        ],
        [
            columns_spec(DSTEP), columns_spec(DSTEP),
            per_head(HD, HD, step=DSTEP), per_head(8, HD, step=DSTEP),
        ],
        [jax.ShapeDtypeStruct((ROWS, HEADS * HD), bf16)] * 2
        + [jax.ShapeDtypeStruct((HEADS, HD, HD), f32), jax.ShapeDtypeStruct((HEADS, 8, HD), f32)],
        mib=24,
        step=DSTEP,
    )(mine, other, squares, *reach)


def inner_kernel(gh_ref, gl_ref, bh_ref, bl_ref, y_ref):
    for n in range(DSTEP):
        at = slice(HD * n, HD * (n + 1))
        grad = gh_ref[:, at], gl_ref[:, at]
        for j in range(NB):
            lo, hi = BLK * j, BLK * (j + 1)
            y_ref[n, lo:hi, :] = mm3(block_column((bh_ref, bl_ref), n, j, j), rows_of(grad, lo, ROWS), TN)


def inner_grad(grad, through):
    return heads_call(
        inner_kernel, "update_grad_local", 4,
        [
            columns_spec(DSTEP), columns_spec(DSTEP),
            per_head(*TRI, step=DSTEP), per_head(*TRI, step=DSTEP),
        ],
        per_head(ROWS, HD, step=DSTEP),
        jax.ShapeDtypeStruct((HEADS, ROWS, HD), f32),
        step=DSTEP,
    )(*grad, *through)


def query_grad_kernel(
    gh_ref, gl_ref, nh_ref, nl_ref, row_ref, ukh_ref, ukl_ref, uqh_ref, uql_ref,
    cols_ref, inverse_ref, state_ref, q_ref, grad_ref, key_ref,
):
    for n in range(STEP):
        at = slice(HD * n, HD * (n + 1))
        grad = gh_ref[:, at], gl_ref[:, at]
        updates = loaded((nh_ref, nl_ref), n)
        uks, uqs = loaded((ukh_ref, ukl_ref), n), loaded((uqh_ref, uql_ref), n)
        from_state = column_of(cols_ref, n, GROWTH) * mm3(grad, split(state_ref[n]), NN)
        none = (jnp.zeros((BLK, BLK), bf16),) * 2
        blocks = [[none] * NB for _ in range(NB)]
        for i in range(NB):
            lo, hi = BLK * i, BLK * (i + 1)
            outer = mm3(rows_of(grad, lo, hi), rows_of(updates, 0, hi), NT)
            scaled = outer * decays(column_of(cols_ref, n, COLUMN), row_ref[n], i)
            for j in range(i + 1):
                blocks[i][j] = split(scaled[:, BLK * j : BLK * (j + 1)])
        through = joined(blocks)
        key_ref[n] = mm3(through, uqs, TN)
        uq = uqs[0].astype(f32) + uqs[1].astype(f32)
        query_grad = from_state + mm3(through, uks, NN)
        query_grad = split(through_unit(query_grad, uq, inverse_ref[n, :, :1]))
        q = q_ref[:, at]
        grad_ref[n] = halves(mm(q, beside(*query_grad), TN))


def query_grad_local(grad, updates, row, uk, uq, cols, inverse, state, queries):
    return heads_call(
        query_grad_kernel, "query_grad", 8,
        [
            columns_spec(), columns_spec(), per_head(ROWS, HD), per_head(ROWS, HD), per_head(1, ROWS),
            per_head(ROWS, HD), per_head(ROWS, HD), per_head(ROWS, HD), per_head(ROWS, HD),
            per_head(ROWS, 8), per_head(ROWS, 8), per_head(HD, HD), columns_spec(),
        ],
        [per_head(HD, HD), per_head(ROWS, HD)],
        [
            jax.ShapeDtypeStruct((HEADS, HD, HD), f32),
            jax.ShapeDtypeStruct((HEADS, ROWS, HD), f32),
        ],
    )(*grad, *updates, row, *uk, *uq, cols, inverse, state, queries)


def key_grad_kernel(
    y_ref, th_ref, tl_ref, nh_ref, nl_ref, row_ref, ukh_ref, ukl_ref,
    cols_ref, state_ref, state_grad_ref, key_ref, k_ref, grad_ref,
):
    for n in range(STEP):
        updates, uks = loaded((nh_ref, nl_ref), n), loaded((ukh_ref, ukl_ref), n)
        state_grad = split(state_grad_ref[n])
        inner = split(y_ref[n] + mm3(loaded((th_ref, tl_ref), n), state_grad, NT))
        write = column_of(cols_ref, n, WRITE)
        base = key_ref[n] + column_of(cols_ref, n, TAIL) * mm3(updates, state_grad, NN)
        base = base - column_of(cols_ref, n, WRITE_GROWTH) * mm3(inner, split(state_ref[n]), NN)
        both = [[None] * NB for _ in range(NB)]
        for i in range(NB):
            lo, hi = BLK * i, BLK * (i + 1)
            outer = mm3(rows_of(inner, lo, hi), rows_of(updates, 0, hi), NT)
            scaled = outer * decays(column_of(cols_ref, n, COLUMN), row_ref[n], i) * write[lo:hi]
            through = jnp.where(strict(i), scaled, 0.0)
            for j in range(i):
                part = through[:, BLK * j : BLK * (j + 1)]
                both[i][j], both[j][i] = split(part), split(part.T)
            part = through[:, lo:hi]
            both[i][i] = split(part + part.T)
        key_grad = base - mm3(joined(both), uks, NN)
        uk = uks[0].astype(f32) + uks[1].astype(f32)
        key_grad = split(through_unit(key_grad, uk, column_of(cols_ref, n, INVERSE)))
        grad_ref[n] = halves(mm(k_ref[...], beside(*key_grad), TN))


def key_grad_local(inner, moved, updates, row, uk, cols, state, state_grad, partial, key_mine):
    return heads_call(
        key_grad_kernel, "key_grad", 9,
        [
            per_head(ROWS, HD), per_head(ROWS, HD), per_head(ROWS, HD), per_head(ROWS, HD),
            per_head(ROWS, HD), per_head(1, ROWS), per_head(ROWS, HD), per_head(ROWS, HD),
            per_head(ROWS, 8), per_head(HD, HD), per_head(HD, HD), per_head(ROWS, HD), whole(ROWS, HD),
        ],
        per_head(HD, HD),
        jax.ShapeDtypeStruct((HEADS, HD, HD), f32),
    )(inner, *moved, *updates, row, *uk, cols, state, state_grad, partial, key_mine)


def exponent_of(largest):
    return jnp.clip(14.0 - jnp.ceil(jnp.log2(jnp.maximum(largest, 1e-30))), -100.0, 100.0)


def summed(pieces):
    exponents = pieces[:, -1:, :].astype(f32)
    exponent = jnp.min(exponents, axis=0) - 3.0
    total = jnp.sum(pieces.astype(f32) * jnp.exp2(exponent[None] - exponents), axis=0)
    return total[:-PAD].astype(f16), jnp.broadcast_to(exponent, (PAD, PIECE)).astype(f16)


def rescaled(message):
    exponent = message[:, -2 * PAD :: PAD, :].astype(f32)
    at = lax.broadcasted_iota(jnp.int32, message.shape, 1)
    scale = jnp.exp2(-exponent)
    return message.astype(f32) * jnp.where(at < HALF, scale[:, :1], scale[:, 1:])


def transpose_over(x, axis, groups=None):
    return lax.all_to_all(x, axis, 0, 0, axis_index_groups=groups, tiled=True)


def shards(queries, key_heads, values, log_decay, write_strength, query_map, key_map, out_weight):
    ctx = lax.axis_index("ctx")
    head_index = lax.axis_index("head")
    core = lax.rem(head_index, 2)
    kv_column = head_index * HEADS // (QUERY_HEAD_COUNT // KVH) * HD
    key_mine = lax.dynamic_slice_in_dim(key_heads, kv_column, HD, 1)
    value_mine = lax.dynamic_slice_in_dim(values, kv_column, HD, 1)
    kv = lax.all_gather(
        jnp.concatenate([key_mine, value_mine], axis=1), "ctx", axis=0, tiled=True
    )
    partner = [(i, i ^ 1) for i in range(2 * CHIPS)]
    w_other = lax.ppermute(out_weight, "head", partner)
    cols, row, *pairs, message = student_keys(
        key_mine, value_mine, log_decay, write_strength, key_map
    )
    uk, lower, inverse, solved = [pairs[2 * i : 2 * i + 2] for i in range(4)]
    ctx_scalar = ctx.astype(jnp.int32).reshape(1)
    core_scalar = core.astype(jnp.int32).reshape(1)
    messages = transpose_over(message, "ctx")
    cols_after, _ = lax.optimization_barrier((cols, message))
    q_inverse, *pairs = student_queries(queries, query_map, cols_after, row, uk, solved)
    uq, attend, own, reach = pairs[:2], pairs[2:4], pairs[4], pairs[5:]
    messages, own = lax.optimization_barrier((messages, own))
    states = chain(messages)
    state = transpose_over(states, "ctx").reshape(HEADS, HD, HD)
    kv, ctx_scalar, _ = lax.optimization_barrier((kv, ctx_scalar, states))
    sent, message_out = [], states
    for half in range(2):
        kv, ctx_scalar, _ = lax.optimization_barrier((kv, ctx_scalar, message_out))
        teacher = teacher_out(half, ctx_scalar, queries, kv)
        state_here, teacher = lax.optimization_barrier((state, teacher))
        delta = student_delta(half, own, reach, state_here, teacher)
        delta_other = lax.ppermute(delta, "head", partner)
        part = project(half, core_scalar, delta, delta_other, out_weight, w_other)
        message_out = part.astype(f16)
        sent.append(transpose_over(message_out, "head", SAME_CORE))
    state_after, _ = lax.optimization_barrier((state, message_out))
    *pairs, = student_ready(solved, lower, inverse, uk, cols, state_after, attend)
    sent[1], pairs = lax.optimization_barrier((sent[1], pairs))
    updates, moved, through = pairs[:2], pairs[2:4], pairs[4:]
    first, second = [summed(pieces) for pieces in sent]
    gathered = lax.all_gather(
        jnp.concatenate([first[0], second[0], first[1], second[1]], axis=0),
        "head", axis=0, axis_index_groups=SAME_CORE, tiled=False,
    )
    columns_high, columns_low = split(rescaled(gathered))
    grad_mine, grad_other, squares = back_project(
        core_scalar, columns_high, columns_low, out_weight, w_other
    )
    grad_high, grad_low, local, squares = state_grad_local(
        grad_mine, lax.ppermute(grad_other, "head", partner), squares, reach
    )
    locals_ = transpose_over(local.reshape(CTX, HD // 2, HD), "ctx")
    (grad_high, grad_low), _ = lax.optimization_barrier(((grad_high, grad_low), local))
    head_grad = [grad_high, grad_low]
    query_grad, partial = query_grad_local(
        head_grad, updates, row, uk, uq, cols, q_inverse, state, queries
    )
    locals_, partial = lax.optimization_barrier((locals_, partial))
    states_back = back_chain(messages, locals_)
    state_grad = transpose_over(states_back, "ctx").reshape(HEADS, HD, HD)
    through_after, _ = lax.optimization_barrier((through, states_back))
    inner = inner_grad(head_grad, through_after)
    key_grad = key_grad_local(
        inner, moved, updates, row, uk, cols, state, state_grad, partial, key_mine
    )
    grads = jnp.concatenate([query_grad, key_grad], axis=0)
    extra = jnp.concatenate([squares, squares], axis=0)
    shared = transpose_over(jnp.concatenate([grads, extra], axis=1), "ctx")
    total = jnp.sum(shared, axis=0, keepdims=True)
    final = transpose_over(jnp.broadcast_to(total, (CTX,) + total.shape[1:]), "ctx")
    normalizer = CTX * ROWS * D
    return jnp.sum(final[:HEADS, HD:]) / normalizer, final[:HEADS, :HD], final[HEADS:, :HD]


def solution(mesh):
    placed = (
        P("ctx", "head"),
        P("ctx", None),
        P("ctx", None),
        P("ctx", "head"),
        P("ctx", "head"),
        P("head", None, None),
        P("head", None, None),
        P("head", None),
    )
    return jax.shard_map(
        shards,
        mesh=mesh,
        in_specs=placed,
        out_specs=(P(), P("head", None, None), P("head", None, None)),
        check_vma=False,
    )
```

```python
import functools
import math

import jax
import jax.numpy as jnp
from jax import lax
from jax.experimental import pallas as pl
from jax.experimental.pallas import tpu as pltpu
from jax.sharding import PartitionSpec as P

D = 8192
QUERY_HEAD_COUNT = 64
KVH = 8
HD = 128
ROWS = 512
BLK = 128
NB = ROWS // BLK
TRI = (2 * BLK, 5 * BLK)
HEADS = 4
CTX = 8
CHIPS = 8
PIECE = 512
PAD = 8
SAME_CORE = [[2 * p + core for p in range(CHIPS)] for core in range(2)]

f32 = jnp.float32
bf16 = jnp.bfloat16
f16 = jnp.float16

MIB = 1024 * 1024
FLOOR = 0
PROJECT_MIB = 45
BACK_MIB = 44
PSTEP = 2
STEP = 1
HALF = ROWS // 2
KSTEP = 4
DSTEP = 2
TEACH = 4


def params(mib):
    return pltpu.CompilerParams(vmem_limit_bytes=max(mib, FLOOR) * MIB)


def cost(micros):
    return pl.CostEstimate(flops=int(micros * 1.1e9), bytes_accessed=0, transcendentals=0)


def split(x):
    high = x.astype(bf16)
    return high, (x - high.astype(f32)).astype(bf16)


NN = (((1,), (0,)), ((), ()))
NT = (((1,), (1,)), ((), ()))
TN = (((0,), (0,)), ((), ()))


def mm(a, b, dims):
    return lax.dot_general(a, b, dims, preferred_element_type=f32)


def beside(a, b):
    return jnp.concatenate([a, b], axis=1)


def above(a, b):
    return jnp.concatenate([a, b], axis=0)


def halves(x):
    n = x.shape[1] // 2
    return x[:, :n] + x[:, n:]


def mm3(a, b, dims):
    depth_at = dims[0][0][0]
    depth = a[0].shape[depth_at]
    if depth <= 128:
        left = beside(*a) if depth_at == 1 else above(*a)
        if dims is NT:
            return halves(mm(left, above(beside(b[0], b[0]), beside(b[1], b[1])), dims))
        if b[0].shape[1] <= 128:
            wide = beside(*b)
            return halves(mm(left, above(wide, wide), dims))
        return mm(left, above(b[0], b[0]), dims) + mm(a[0], b[1], dims)
    if dims is not NT and b[0].shape[1] <= 128:
        return halves(mm(a[0], beside(*b), dims)) + mm(a[1], b[0], dims)
    return mm(a[0], b[0], dims) + (mm(a[0], b[1], dims) + mm(a[1], b[0], dims))


def rows_of(pair, lo, hi):
    return pair[0][lo:hi], pair[1][lo:hi]


def stack(a, b):
    return above(a[0], b[0]), above(a[1], b[1])


PACKED = ((0, 4 * BLK), (BLK, 3 * BLK), (BLK, 0), (0, 0))


def block(refs, n, i, j):
    at, left = PACKED[i]
    return tuple(ref[n, at : at + BLK, left + BLK * j : left + BLK * (j + 1)] for ref in refs)


def block_column(refs, n, j, first):
    parts = []
    for ref in refs:
        blocks = []
        for i in range(first, NB):
            at, left = PACKED[i]
            blocks.append(ref[n, at : at + BLK, left + BLK * j : left + BLK * (j + 1)])
        parts.append(jnp.concatenate(blocks, axis=0))
    return tuple(parts)


def store_row(refs, n, i, pair):
    at, left = PACKED[i]
    for ref, part in zip(refs, pair):
        ref[n, at : at + BLK, left : left + BLK * (i + 1)] = part


def joined(blocks):
    return tuple(
        jnp.concatenate([jnp.concatenate([b[p] for b in line], axis=1) for line in blocks], axis=0)
        for p in range(2)
    )


def loaded(refs, n):
    return refs[0][n], refs[1][n]


def store(refs, n, pair):
    refs[0][n] = pair[0]
    refs[1][n] = pair[1]


def unit(x):
    inverse = 1.0 / jnp.sqrt(jnp.sum(x * x, axis=-1, keepdims=True) + 1e-06)
    return x * inverse, inverse


def through_unit(grad, units, inverse):
    return inverse * (grad - units * jnp.sum(units * grad, axis=1, keepdims=True))


def gate_forms(gate_row, write_row):
    ii = lax.broadcasted_iota(jnp.int32, (ROWS, ROWS), 0)
    jj = lax.broadcasted_iota(jnp.int32, (ROWS, ROWS), 1)
    gate = jnp.sum(jnp.where(ii == jj, gate_row, 0.0), axis=1, keepdims=True)
    write = jnp.sum(jnp.where(ii == jj, write_row, 0.0), axis=1, keepdims=True)
    column = jnp.sum(jnp.where(jj <= ii, gate_row, 0.0), axis=1, keepdims=True)
    row = jnp.sum(jnp.where(ii <= jj, gate, 0.0), axis=0, keepdims=True)
    return column, row, write


def decays(column, row, i):
    width = BLK * (i + 1)
    ii = lax.broadcasted_iota(jnp.int32, (BLK, width), 0) + BLK * i
    jj = lax.broadcasted_iota(jnp.int32, (BLK, width), 1)
    inclusive = ii >= jj
    gap = column[BLK * i : width] - row[:, :width]
    return jnp.where(inclusive, jnp.exp(jnp.where(inclusive, gap, 0.0)), 0.0)


def strict(i):
    width = BLK * (i + 1)
    ii = lax.broadcasted_iota(jnp.int32, (BLK, width), 0) + BLK * i
    return ii > lax.broadcasted_iota(jnp.int32, (BLK, width), 1)


def inverses(blocks):
    ii = lax.broadcasted_iota(jnp.int32, (BLK, BLK), 0)
    jj = lax.broadcasted_iota(jnp.int32, (BLK, BLK), 1)
    diagonal = (ii == jj).astype(f32)
    first = ((ii >> 1) == (jj >> 1)) & (ii > jj)
    found = [split(diagonal - jnp.where(first, block, 0.0)) for block in blocks]
    whole_parts = [split(-block) for block in blocks]
    none = jnp.zeros((BLK, BLK), bf16)
    shift = 1
    while (1 << shift) < BLK:
        mask = ((ii >> (shift + 1)) == (jj >> (shift + 1))) & ((ii >> shift) > (jj >> shift))
        corner = [tuple(jnp.where(mask, part, none) for part in pair) for pair in whole_parts]
        inner = [split(mm3(c, x, NN)) for c, x in zip(corner, found)]
        more = [split(mm3(x, y, NN)) for x, y in zip(found, inner)]
        found = [(x[0] + y[0], x[1] + y[1]) for x, y in zip(found, more)]
        shift += 1
    return found


GROWTH, TAIL, WRITE, WRITE_GROWTH, INVERSE, COLUMN = range(6)


def column_of(ref, n, which):
    return ref[n, :, which : which + 1]


def per_head(*shape, step=None):
    return pl.BlockSpec((step or STEP,) + shape, lambda h, *_: (h,) + (0,) * len(shape))


def whole(*shape):
    return pl.BlockSpec(shape, lambda h, *_: (0,) * len(shape))


def columns_spec(step=None):
    return pl.BlockSpec((ROWS, (step or STEP) * HD), lambda h, *_: (0, h))


def pair_shape(*shape):
    return [jax.ShapeDtypeStruct((HEADS,) + shape, bf16)] * 2


def heads_call(kernel, name, micros, in_specs, out_specs, out_shape, mib=56, step=None):
    return pl.pallas_call(
        kernel,
        grid=(HEADS // (step or STEP),),
        in_specs=in_specs,
        out_specs=out_specs,
        out_shape=out_shape,
        compiler_params=params(mib),
        cost_estimate=cost(micros),
        name=name,
    )


def keys_kernel(
    k_ref, v_ref, gate_ref, write_ref, kmap_ref,
    cols_ref, row_ref, ukh_ref, ukl_ref, lh_ref, ll_ref, dh_ref, dl_ref, xh_ref, xl_ref, message_ref,
):
    heads = range(KSTEP)
    lower, uks, columns, rights, ends = [], [], [], [], []
    for n in heads:
        column, row, write = gate_forms(
            gate_ref[pl.ds(pl.program_id(0) * KSTEP + n, 1), :],
            write_ref[pl.ds(pl.program_id(0) * KSTEP + n, 1), :],
        )
        end = row[:, ROWS - 1 : ROWS]
        growth = jnp.exp(column)
        tail = jnp.exp(end - column)
        uk, inverse = unit(mm(k_ref[...], kmap_ref[n], NN))
        pair = split(uk)
        store((ukh_ref, ukl_ref), n, pair)
        for which, value in enumerate((growth, tail, write, write * growth, inverse, column)):
            cols_ref[n, :, which : which + 1] = value
        row_ref[n] = row
        own = []
        for i in range(NB):
            lo, hi = BLK * i, BLK * (i + 1)
            gram = mm3(rows_of(pair, lo, hi), rows_of(pair, 0, hi), NT)
            decay = decays(column, row, i)
            own.append(jnp.where(strict(i), gram * decay * write[lo:hi], 0.0))
        lower.append(own)
        uks.append(split(tail * uk))
        rights.append(beside(write * v_ref[...].astype(f32), (write * growth) * uk))
        ends.append(end)
    found = inverses([lower[n][i][:, BLK * i :] for n in heads for i in range(NB)])
    inverse = [[found[n * NB + i] for i in range(NB)] for n in heads]
    solved = [None] * KSTEP
    for i in range(NB):
        lo, hi = BLK * i, BLK * (i + 1)
        for n in heads:
            low = split(lower[n][i])
            store_row((lh_ref, ll_ref), n, i, low)
            dh_ref[n, lo:hi, :] = inverse[n][i][0]
            dl_ref[n, lo:hi, :] = inverse[n][i][1]
            rest = rights[n][lo:hi]
            if i:
                rest = rest - mm3((low[0][:, :lo], low[1][:, :lo]), solved[n], NN)
            x = split(mm3(inverse[n][i], split(rest), NN))
            solved[n] = stack(solved[n], x) if i else x
    ii = lax.broadcasted_iota(jnp.int32, (HD, HD), 0)
    jj = lax.broadcasted_iota(jnp.int32, (HD, HD), 1)
    half = HD // 2
    for n in heads:
        store((xh_ref, xl_ref), n, solved[n])
        moved = mm3(solved[n], uks[n], TN)
        carry = jnp.where(ii == jj, jnp.exp(ends[n]), 0.0) - moved[HD:]
        for s in range(2):
            message_ref[2 * n + s, :half, :] = moved[half * s : half * (s + 1)]
            message_ref[2 * n + s, half:, :] = carry


def student_keys(key_mine, value_mine, log_decay, write_strength, key_map):
    return heads_call(
        keys_kernel, "student_keys", 16,
        [whole(ROWS, HD), whole(ROWS, HD), whole(HEADS, ROWS), whole(HEADS, ROWS), per_head(HD, HD, step=KSTEP)],
        [
            per_head(ROWS, 8, step=KSTEP), per_head(1, ROWS, step=KSTEP),
            per_head(ROWS, HD, step=KSTEP), per_head(ROWS, HD, step=KSTEP),
            per_head(*TRI, step=KSTEP), per_head(*TRI, step=KSTEP),
            per_head(ROWS, BLK, step=KSTEP), per_head(ROWS, BLK, step=KSTEP),
            per_head(ROWS, 2 * HD, step=KSTEP), per_head(ROWS, 2 * HD, step=KSTEP),
            pl.BlockSpec((2 * KSTEP, HD + HD // 2, HD), lambda h: (h, 0, 0)),
        ],
        [
            jax.ShapeDtypeStruct((HEADS, ROWS, 8), f32),
            jax.ShapeDtypeStruct((HEADS, 1, ROWS), f32),
            *pair_shape(ROWS, HD), *pair_shape(*TRI), *pair_shape(ROWS, BLK), *pair_shape(ROWS, 2 * HD),
            jax.ShapeDtypeStruct((2 * HEADS, HD + HD // 2, HD), f32),
        ],
        step=KSTEP,
    )(key_mine, value_mine, log_decay.T, write_strength.T, key_map)


def queries_kernel(
    q_ref, qmap_ref, cols_ref, row_ref, ukh_ref, ukl_ref, xh_ref, xl_ref,
    inverse_ref, uqh_ref, uql_ref, ah_ref, al_ref, own_ref, rh_ref, rl_ref,
):
    for n in range(STEP):
        uq, inverse = unit(mm(q_ref[:, HD * n : HD * (n + 1)], qmap_ref[n], NN))
        inverse_ref[n, :, :1] = inverse
        uqs = split(uq)
        store((uqh_ref, uql_ref), n, uqs)
        uks = loaded((ukh_ref, ukl_ref), n)
        solved = loaded((xh_ref, xl_ref), n)
        reach = column_of(cols_ref, n, GROWTH) * uq
        for i in range(NB):
            lo, hi = BLK * i, BLK * (i + 1)
            decay = decays(column_of(cols_ref, n, COLUMN), row_ref[n], i)
            attend = split(mm3(rows_of(uqs, lo, hi), rows_of(uks, 0, hi), NT) * decay)
            store_row((ah_ref, al_ref), n, i, attend)
            z = mm3(attend, rows_of(solved, 0, hi), NN)
            own_ref[n, lo:hi, :] = z[:, :HD]
            part = split(reach[lo:hi] - z[:, HD:])
            rh_ref[n, lo:hi, :] = part[0]
            rl_ref[n, lo:hi, :] = part[1]


def student_queries(queries, query_map, cols, row, uk, solved):
    return heads_call(
        queries_kernel, "student_queries", 8,
        [
            columns_spec(), per_head(HD, HD), per_head(ROWS, 8), per_head(1, ROWS),
            per_head(ROWS, HD), per_head(ROWS, HD), per_head(ROWS, 2 * HD), per_head(ROWS, 2 * HD),
        ],
        [
            per_head(ROWS, 8), per_head(ROWS, HD), per_head(ROWS, HD), per_head(*TRI),
            per_head(*TRI), per_head(ROWS, HD), per_head(ROWS, HD), per_head(ROWS, HD),
        ],
        [
            jax.ShapeDtypeStruct((HEADS, ROWS, 8), f32),
            *pair_shape(ROWS, HD), *pair_shape(*TRI),
            jax.ShapeDtypeStruct((HEADS, ROWS, HD), f32),
            *pair_shape(ROWS, HD),
        ],
    )(queries, query_map, cols, row, *uk, *solved)


def chain_kernel(message_ref, out_ref):
    half = HD // 2
    carries = [split(message_ref[c, half:, :]) for c in range(CTX - 1)]
    state = jnp.zeros((half, HD), f32)
    out_ref[0] = state
    for c in range(CTX - 1):
        state = mm3(split(state), carries[c], NN) + message_ref[c, :half, :]
        out_ref[c + 1] = state


def chain(messages):
    return pl.pallas_call(
        chain_kernel,
        out_shape=jax.ShapeDtypeStruct((CTX, HD // 2, HD), f32),
        compiler_params=params(8),
        cost_estimate=cost(3),
        name="state_chain",
    )(messages)


def back_chain_kernel(message_ref, grad_ref, out_ref):
    half = HD // 2
    carries = [split(message_ref[c, half:, :]) for c in range(CTX)]
    state = jnp.zeros((half, HD), f32)
    out_ref[CTX - 1] = state
    for c in range(CTX - 1, 0, -1):
        state = mm3(split(state), carries[c], NT) + grad_ref[c]
        out_ref[c - 1] = state


def back_chain(messages, grads):
    return pl.pallas_call(
        back_chain_kernel,
        out_shape=jax.ShapeDtypeStruct((CTX, HD // 2, HD), f32),
        compiler_params=params(8),
        cost_estimate=cost(3),
        name="state_grad_chain",
    )(messages, grads)


def teacher_kernel(half, ctx_ref, q_ref, kv_ref, out_ref):
    mine = ctx_ref[0]
    scale = math.log2(math.e) / math.sqrt(HD)

    def block(j, carry, width, diagonal):
        start = pl.multiple_of(j * ROWS, ROWS)
        keys = kv_ref[pl.ds(start, width), :HD]
        values = kv_ref[pl.ds(start, width), HD:]
        out = []
        raw = [mm(q_ref[:, HD * n : HD * (n + 1)], keys, NT) for n in range(TEACH)]
        for n in range(TEACH):
            top, total, mixed = carry[n]
            scores = raw[n]
            if diagonal:
                ii = lax.broadcasted_iota(jnp.int32, (HALF, width), 0) + HALF * half
                jj = lax.broadcasted_iota(jnp.int32, (HALF, width), 1)
                scores = jnp.where(jj <= ii, scores, -jnp.inf)
            new_top = jnp.maximum(top, jnp.max(scores, axis=1, keepdims=True))
            fade = jnp.exp2((top - new_top) * scale)
            weights = jnp.exp2((scores - new_top) * scale)
            total = total * fade + jnp.sum(weights, axis=1, keepdims=True)
            mixed = mixed * fade + mm(weights.astype(bf16), values, NN)
            out.append((new_top, total, mixed))
        return tuple(out)

    start = (
        jnp.full((HALF, 1), -jnp.inf, f32),
        jnp.zeros((HALF, 1), f32),
        jnp.zeros((HALF, HD), f32),
    )
    carry = block(mine, (start,) * TEACH, HALF * (half + 1), True)
    carry = lax.fori_loop(0, mine, lambda j, c: block(j, c, ROWS, False), carry)
    for n in range(TEACH):
        _, total, mixed = carry[n]
        out_ref[:, HD * n : HD * (n + 1)] = (mixed / total).astype(bf16)


def teacher_out(half, ctx, queries, kv):
    return pl.pallas_call(
        functools.partial(teacher_kernel, half),
        grid_spec=pltpu.PrefetchScalarGridSpec(
            num_scalar_prefetch=1,
            grid=(HEADS // TEACH,),
            in_specs=[
                pl.BlockSpec((HALF, TEACH * HD), lambda h, c: (half, h)),
                pl.BlockSpec((CTX * ROWS, 2 * HD), lambda h, c: (0, 0)),
            ],
            out_specs=pl.BlockSpec((HALF, TEACH * HD), lambda h, c: (0, h)),
        ),
        out_shape=jax.ShapeDtypeStruct((HALF, HEADS * HD), bf16),
        compiler_params=params(24),
        cost_estimate=cost(9),
        name=f"teacher_{half}",
    )(ctx, queries, kv)


def delta_kernel(own_ref, rh_ref, rl_ref, state_ref, teacher_ref, delta_ref):
    for n in range(DSTEP):
        student = own_ref[n] + mm3(loaded((rh_ref, rl_ref), n), split(state_ref[n]), NT)
        delta = split(student - teacher_ref[:, HD * n : HD * (n + 1)].astype(f32))
        delta_ref[0, :, HD * n : HD * (n + 1)] = delta[0]
        delta_ref[1, :, HD * n : HD * (n + 1)] = delta[1]


def student_delta(half, own, reach, state, teacher):
    rows = pl.BlockSpec((DSTEP, HALF, HD), lambda h: (h, half, 0))
    return heads_call(
        delta_kernel, f"delta_{half}", 2,
        [rows, rows, rows, per_head(HD, HD, step=DSTEP), pl.BlockSpec((HALF, DSTEP * HD), lambda h: (0, h))],
        pl.BlockSpec((2, HALF, DSTEP * HD), lambda h: (0, 0, h)),
        jax.ShapeDtypeStruct((2, HALF, HEADS * HD), bf16),
        mib=24,
        step=DSTEP,
    )(own, *reach, state, teacher)


def solve_back(refs_l, refs_d, n, right):
    solved, out = None, []
    for j in range(NB - 1, -1, -1):
        lo, hi = BLK * j, BLK * (j + 1)
        rest = right[j]
        if solved is not None:
            rest = rest - mm3(block_column(refs_l, n, j, j + 1), solved, TN)
        y = mm3((refs_d[0][n, lo:hi, :], refs_d[1][n, lo:hi, :]), split(rest), TN)
        out.append(y)
        solved = split(y) if solved is None else stack(split(y), solved)
    return solved, out[::-1]


def ready_kernel(
    xh_ref, xl_ref, lh_ref, ll_ref, dh_ref, dl_ref, ukh_ref, ukl_ref, cols_ref, state_ref, ah_ref, al_ref,
    nh_ref, nl_ref, th_ref, tl_ref, bh_ref, bl_ref,
):
    for n in range(STEP):
        found = [None] * NB
        for j in range(NB - 1, -1, -1):
            rest = block_column((ah_ref, al_ref), n, j, j)
            if j < NB - 1:
                rest = rest[0].astype(f32) + rest[1].astype(f32)
                for i in range(j + 1, NB):
                    more = mm3(found[i], block((lh_ref, ll_ref), n, i, j), NN)
                    at = BLK * (i - j)
                    rest = jnp.concatenate([rest[:at], rest[at:] - more], axis=0)
                rest = split(rest)
            d = dh_ref[n, BLK * j : BLK * (j + 1), :], dl_ref[n, BLK * j : BLK * (j + 1), :]
            found[j] = split(mm3(rest, d, NN))
            for i in range(j, NB):
                at, left = PACKED[i]
                for ref, part in zip((bh_ref, bl_ref), found[j]):
                    ref[n, at : at + BLK, left + BLK * j : left + BLK * (j + 1)] = part[BLK * (i - j) : BLK * (i - j + 1)]
        x = loaded((xh_ref, xl_ref), n)
        state = split(state_ref[n])
        first = x[0][:, :HD].astype(f32) + x[1][:, :HD].astype(f32)
        store((nh_ref, nl_ref), n, split(first - mm3((x[0][:, HD:], x[1][:, HD:]), state, NT)))
        uk = ukh_ref[n].astype(f32) + ukl_ref[n].astype(f32)
        moved = column_of(cols_ref, n, TAIL) * uk
        solved, _ = solve_back(
            (lh_ref, ll_ref), (dh_ref, dl_ref), n, [moved[BLK * j : BLK * (j + 1)] for j in range(NB)]
        )
        store((th_ref, tl_ref), n, solved)


def student_ready(solved, lower, inverse, uk, cols, state, attend):
    return heads_call(
        ready_kernel, "backward_ready", 10,
        [
            per_head(ROWS, 2 * HD), per_head(ROWS, 2 * HD), per_head(*TRI), per_head(*TRI),
            per_head(ROWS, BLK), per_head(ROWS, BLK), per_head(ROWS, HD), per_head(ROWS, HD),
            per_head(ROWS, 8), per_head(HD, HD), per_head(*TRI), per_head(*TRI),
        ],
        [per_head(ROWS, HD)] * 4 + [per_head(*TRI)] * 2,
        pair_shape(ROWS, HD) + pair_shape(ROWS, HD) + pair_shape(*TRI),
    )(*solved, *lower, *inverse, *uk, cols, state, *attend)


def project_kernel(core_ref, mine_ref, other_ref, w_mine_ref, w_other_ref, out_ref):
    width = HEADS * HD
    both = mm(mine_ref[...].reshape(2 * HALF, width), w_mine_ref[...], NN)
    both = both + mm(other_ref[...].reshape(2 * HALF, width), w_other_ref[...], NN)
    total = both[:HALF] + both[HALF:]
    largest = jnp.max(jnp.max(jnp.abs(total), axis=1, keepdims=True), axis=0, keepdims=True)
    exponent = exponent_of(largest)
    scaled = total * jnp.exp2(exponent)
    for p in range(PSTEP):
        at = slice(PIECE * p, PIECE * (p + 1))
        out_ref[p, :HALF, :] = scaled[:, at]
        out_ref[p, HALF:, :] = jnp.broadcast_to(exponent, (PAD, PIECE))


def project(half, core, mine, other, w_mine, w_other):
    width = HEADS * HD
    return pl.pallas_call(
        project_kernel,
        grid_spec=pltpu.PrefetchScalarGridSpec(
            num_scalar_prefetch=1,
            grid=(CHIPS // PSTEP,),
            in_specs=[
                pl.BlockSpec((2, HALF, width), lambda j, c: (0, 0, 0)),
                pl.BlockSpec((2, HALF, width), lambda j, c: (0, 0, 0)),
                pl.BlockSpec((width, PSTEP * PIECE), lambda j, c: (0, c[0] * (CHIPS // PSTEP) + j)),
                pl.BlockSpec((width, PSTEP * PIECE), lambda j, c: (0, c[0] * (CHIPS // PSTEP) + j)),
            ],
            out_specs=pl.BlockSpec((PSTEP, HALF + PAD, PIECE), lambda j, c: (j, 0, 0)),
        ),
        out_shape=jax.ShapeDtypeStruct((CHIPS, HALF + PAD, PIECE), f32),
        compiler_params=params(PROJECT_MIB),
        cost_estimate=cost(7),
        name=f"difference_part_{half}",
    )(core, mine, other, w_mine, w_other)


def back_project_kernel(
    core_ref, high_ref, low_ref, w_mine_ref, w_other_ref, mine_ref, other_ref, square_ref
):
    mine = other = square = 0.0
    for p in range(PSTEP):
        at = slice(PIECE * p, PIECE * (p + 1))
        both = jnp.concatenate([high_ref[p, :ROWS, :], low_ref[p, :ROWS, :]], axis=0)
        mine = mine + mm(both, w_mine_ref[:, at], NT)
        other = other + mm(both, w_other_ref[:, at], NT)
        values = both[:ROWS].astype(f32) + both[ROWS:].astype(f32)
        square = square + jnp.sum((values * values).reshape(ROWS // 8, 8, PIECE), axis=0)
    mine = mine[:ROWS] + mine[ROWS:]
    other = other[:ROWS] + other[ROWS:]

    @pl.when(pl.program_id(0) == 0)
    def _():
        mine_ref[...] = mine
        other_ref[:ROWS, :] = other
        other_ref[ROWS:, :] = square
        square_ref[...] = square

    @pl.when(pl.program_id(0) > 0)
    def _():
        mine_ref[...] += mine
        other_ref[:ROWS, :] += other
        other_ref[ROWS:, :] += square
        square_ref[...] += square


def back_project(core, high, low, w_mine, w_other):
    width = HEADS * HD
    columns = pl.BlockSpec((PSTEP, ROWS + 2 * PAD, PIECE), lambda j, c: (j, 0, 0))
    return pl.pallas_call(
        back_project_kernel,
        grid_spec=pltpu.PrefetchScalarGridSpec(
            num_scalar_prefetch=1,
            grid=(CHIPS // PSTEP,),
            in_specs=[
                columns,
                columns,
                pl.BlockSpec((width, PSTEP * PIECE), lambda j, c: (0, c[0] * (CHIPS // PSTEP) + j)),
                pl.BlockSpec((width, PSTEP * PIECE), lambda j, c: (0, c[0] * (CHIPS // PSTEP) + j)),
            ],
            out_specs=[
                pl.BlockSpec((ROWS, width), lambda j, c: (0, 0)),
                pl.BlockSpec((ROWS + 8, width), lambda j, c: (0, 0)),
                pl.BlockSpec((8, PIECE), lambda j, c: (0, 0)),
            ],
        ),
        out_shape=[
            jax.ShapeDtypeStruct((ROWS, width), f32),
            jax.ShapeDtypeStruct((ROWS + 8, width), f32),
            jax.ShapeDtypeStruct((8, PIECE), f32),
        ],
        compiler_params=params(BACK_MIB),
        cost_estimate=cost(14),
        name="head_grad_part",
    )(core, high, low, w_mine, w_other)


def state_grad_kernel(
    mine_ref, other_ref, square_ref, rh_ref, rl_ref, gh_ref, gl_ref, out_ref, total_ref
):
    for n in range(DSTEP):
        at = slice(HD * n, HD * (n + 1))
        grad = split(mine_ref[:, at] + other_ref[:ROWS, at])
        gh_ref[:, at] = grad[0]
        gl_ref[:, at] = grad[1]
        out_ref[n] = mm3(grad, loaded((rh_ref, rl_ref), n), TN)
        total_ref[n] = square_ref[:, at] + other_ref[ROWS:, at]


def state_grad_local(mine, other, squares, reach):
    return heads_call(
        state_grad_kernel, "state_grad_local", 2,
        [
            columns_spec(DSTEP),
            pl.BlockSpec((ROWS + 8, DSTEP * HD), lambda h: (0, h)),
            pl.BlockSpec((8, DSTEP * HD), lambda h: (0, h)),
            per_head(ROWS, HD, step=DSTEP), per_head(ROWS, HD, step=DSTEP),
        ],
        [
            columns_spec(DSTEP), columns_spec(DSTEP),
            per_head(HD, HD, step=DSTEP), per_head(8, HD, step=DSTEP),
        ],
        [jax.ShapeDtypeStruct((ROWS, HEADS * HD), bf16)] * 2
        + [jax.ShapeDtypeStruct((HEADS, HD, HD), f32), jax.ShapeDtypeStruct((HEADS, 8, HD), f32)],
        mib=24,
        step=DSTEP,
    )(mine, other, squares, *reach)


def inner_kernel(gh_ref, gl_ref, bh_ref, bl_ref, y_ref):
    for n in range(DSTEP):
        at = slice(HD * n, HD * (n + 1))
        grad = gh_ref[:, at], gl_ref[:, at]
        for j in range(NB):
            lo, hi = BLK * j, BLK * (j + 1)
            y_ref[n, lo:hi, :] = mm3(block_column((bh_ref, bl_ref), n, j, j), rows_of(grad, lo, ROWS), TN)


def inner_grad(grad, through):
    return heads_call(
        inner_kernel, "update_grad_local", 4,
        [
            columns_spec(DSTEP), columns_spec(DSTEP),
            per_head(*TRI, step=DSTEP), per_head(*TRI, step=DSTEP),
        ],
        per_head(ROWS, HD, step=DSTEP),
        jax.ShapeDtypeStruct((HEADS, ROWS, HD), f32),
        step=DSTEP,
    )(*grad, *through)


def query_grad_kernel(
    gh_ref, gl_ref, nh_ref, nl_ref, row_ref, ukh_ref, ukl_ref, uqh_ref, uql_ref,
    cols_ref, inverse_ref, state_ref, q_ref, grad_ref, key_ref,
):
    for n in range(STEP):
        at = slice(HD * n, HD * (n + 1))
        grad = gh_ref[:, at], gl_ref[:, at]
        updates = loaded((nh_ref, nl_ref), n)
        uks, uqs = loaded((ukh_ref, ukl_ref), n), loaded((uqh_ref, uql_ref), n)
        from_state = column_of(cols_ref, n, GROWTH) * mm3(grad, split(state_ref[n]), NN)
        none = (jnp.zeros((BLK, BLK), bf16),) * 2
        blocks = [[none] * NB for _ in range(NB)]
        for i in range(NB):
            lo, hi = BLK * i, BLK * (i + 1)
            outer = mm3(rows_of(grad, lo, hi), rows_of(updates, 0, hi), NT)
            scaled = outer * decays(column_of(cols_ref, n, COLUMN), row_ref[n], i)
            for j in range(i + 1):
                blocks[i][j] = split(scaled[:, BLK * j : BLK * (j + 1)])
        through = joined(blocks)
        key_ref[n] = mm3(through, uqs, TN)
        uq = uqs[0].astype(f32) + uqs[1].astype(f32)
        query_grad = from_state + mm3(through, uks, NN)
        query_grad = split(through_unit(query_grad, uq, inverse_ref[n, :, :1]))
        q = q_ref[:, at]
        grad_ref[n] = halves(mm(q, beside(*query_grad), TN))


def query_grad_local(grad, updates, row, uk, uq, cols, inverse, state, queries):
    return heads_call(
        query_grad_kernel, "query_grad", 8,
        [
            columns_spec(), columns_spec(), per_head(ROWS, HD), per_head(ROWS, HD), per_head(1, ROWS),
            per_head(ROWS, HD), per_head(ROWS, HD), per_head(ROWS, HD), per_head(ROWS, HD),
            per_head(ROWS, 8), per_head(ROWS, 8), per_head(HD, HD), columns_spec(),
        ],
        [per_head(HD, HD), per_head(ROWS, HD)],
        [
            jax.ShapeDtypeStruct((HEADS, HD, HD), f32),
            jax.ShapeDtypeStruct((HEADS, ROWS, HD), f32),
        ],
    )(*grad, *updates, row, *uk, *uq, cols, inverse, state, queries)


def key_grad_kernel(
    y_ref, th_ref, tl_ref, nh_ref, nl_ref, row_ref, ukh_ref, ukl_ref,
    cols_ref, state_ref, state_grad_ref, key_ref, k_ref, grad_ref,
):
    for n in range(STEP):
        updates, uks = loaded((nh_ref, nl_ref), n), loaded((ukh_ref, ukl_ref), n)
        state_grad = split(state_grad_ref[n])
        inner = split(y_ref[n] + mm3(loaded((th_ref, tl_ref), n), state_grad, NT))
        write = column_of(cols_ref, n, WRITE)
        base = key_ref[n] + column_of(cols_ref, n, TAIL) * mm3(updates, state_grad, NN)
        base = base - column_of(cols_ref, n, WRITE_GROWTH) * mm3(inner, split(state_ref[n]), NN)
        both = [[None] * NB for _ in range(NB)]
        for i in range(NB):
            lo, hi = BLK * i, BLK * (i + 1)
            outer = mm3(rows_of(inner, lo, hi), rows_of(updates, 0, hi), NT)
            scaled = outer * decays(column_of(cols_ref, n, COLUMN), row_ref[n], i) * write[lo:hi]
            through = jnp.where(strict(i), scaled, 0.0)
            for j in range(i):
                part = through[:, BLK * j : BLK * (j + 1)]
                both[i][j], both[j][i] = split(part), split(part.T)
            part = through[:, lo:hi]
            both[i][i] = split(part + part.T)
        key_grad = base - mm3(joined(both), uks, NN)
        uk = uks[0].astype(f32) + uks[1].astype(f32)
        key_grad = split(through_unit(key_grad, uk, column_of(cols_ref, n, INVERSE)))
        grad_ref[n] = halves(mm(k_ref[...], beside(*key_grad), TN))


def key_grad_local(inner, moved, updates, row, uk, cols, state, state_grad, partial, key_mine):
    return heads_call(
        key_grad_kernel, "key_grad", 9,
        [
            per_head(ROWS, HD), per_head(ROWS, HD), per_head(ROWS, HD), per_head(ROWS, HD),
            per_head(ROWS, HD), per_head(1, ROWS), per_head(ROWS, HD), per_head(ROWS, HD),
            per_head(ROWS, 8), per_head(HD, HD), per_head(HD, HD), per_head(ROWS, HD), whole(ROWS, HD),
        ],
        per_head(HD, HD),
        jax.ShapeDtypeStruct((HEADS, HD, HD), f32),
    )(inner, *moved, *updates, row, *uk, cols, state, state_grad, partial, key_mine)


def exponent_of(largest):
    return jnp.clip(14.0 - jnp.ceil(jnp.log2(jnp.maximum(largest, 1e-30))), -100.0, 100.0)


def summed(pieces):
    exponents = pieces[:, -1:, :].astype(f32)
    exponent = jnp.min(exponents, axis=0) - 3.0
    total = jnp.sum(pieces.astype(f32) * jnp.exp2(exponent[None] - exponents), axis=0)
    return total[:-PAD].astype(f16), jnp.broadcast_to(exponent, (PAD, PIECE)).astype(f16)


def rescaled(message):
    at = lax.broadcasted_iota(jnp.int32, message.shape, 1)
    first, second = message[:, ROWS : ROWS + 1, :], message[:, ROWS + PAD : ROWS + PAD + 1, :]
    exponent = jnp.where(at < HALF, first, second).astype(f32)
    return message.astype(f32) * jnp.exp2(-exponent)


def transpose_over(x, axis, groups=None):
    return lax.all_to_all(x, axis, 0, 0, axis_index_groups=groups, tiled=True)


def shards(queries, key_heads, values, log_decay, write_strength, query_map, key_map, out_weight):
    ctx = lax.axis_index("ctx")
    head_index = lax.axis_index("head")
    core = lax.rem(head_index, 2)
    kv_column = head_index * HEADS // (QUERY_HEAD_COUNT // KVH) * HD
    key_mine = lax.dynamic_slice_in_dim(key_heads, kv_column, HD, 1)
    value_mine = lax.dynamic_slice_in_dim(values, kv_column, HD, 1)
    kv = lax.all_gather(
        jnp.concatenate([key_mine, value_mine], axis=1), "ctx", axis=0, tiled=True
    )
    partner = [(i, i ^ 1) for i in range(2 * CHIPS)]
    w_other = lax.ppermute(out_weight, "head", partner)
    cols, row, *pairs, message = student_keys(
        key_mine, value_mine, log_decay, write_strength, key_map
    )
    uk, lower, inverse, solved = [pairs[2 * i : 2 * i + 2] for i in range(4)]
    ctx_scalar = ctx.astype(jnp.int32).reshape(1)
    core_scalar = core.astype(jnp.int32).reshape(1)
    messages = transpose_over(message, "ctx")
    cols_after, _ = lax.optimization_barrier((cols, message))
    q_inverse, *pairs = student_queries(queries, query_map, cols_after, row, uk, solved)
    uq, attend, own, reach = pairs[:2], pairs[2:4], pairs[4], pairs[5:]
    messages, own = lax.optimization_barrier((messages, own))
    states = chain(messages)
    state = transpose_over(states, "ctx").reshape(HEADS, HD, HD)
    kv, ctx_scalar, _ = lax.optimization_barrier((kv, ctx_scalar, states))
    sent, message_out = [], states
    for half in range(2):
        kv, ctx_scalar, _ = lax.optimization_barrier((kv, ctx_scalar, message_out))
        teacher = teacher_out(half, ctx_scalar, queries, kv)
        state_here, teacher = lax.optimization_barrier((state, teacher))
        delta = student_delta(half, own, reach, state_here, teacher)
        delta_other = lax.ppermute(delta, "head", partner)
        part = project(half, core_scalar, delta, delta_other, out_weight, w_other)
        message_out = part.astype(f16)
        sent.append(transpose_over(message_out, "head", SAME_CORE))
    state_after, _ = lax.optimization_barrier((state, message_out))
    *pairs, = student_ready(solved, lower, inverse, uk, cols, state_after, attend)
    sent[1], pairs = lax.optimization_barrier((sent[1], pairs))
    updates, moved, through = pairs[:2], pairs[2:4], pairs[4:]
    first, second = [summed(pieces) for pieces in sent]
    gathered = lax.all_gather(
        jnp.concatenate([first[0], second[0], first[1], second[1]], axis=0),
        "head", axis=0, axis_index_groups=SAME_CORE, tiled=False,
    )
    columns_high, columns_low = split(rescaled(gathered))
    grad_mine, grad_other, squares = back_project(
        core_scalar, columns_high, columns_low, out_weight, w_other
    )
    grad_high, grad_low, local, squares = state_grad_local(
        grad_mine, lax.ppermute(grad_other, "head", partner), squares, reach
    )
    locals_ = transpose_over(local.reshape(CTX, HD // 2, HD), "ctx")
    (grad_high, grad_low), _ = lax.optimization_barrier(((grad_high, grad_low), local))
    head_grad = [grad_high, grad_low]
    query_grad, partial = query_grad_local(
        head_grad, updates, row, uk, uq, cols, q_inverse, state, queries
    )
    locals_, partial = lax.optimization_barrier((locals_, partial))
    states_back = back_chain(messages, locals_)
    state_grad = transpose_over(states_back, "ctx").reshape(HEADS, HD, HD)
    through_after, _ = lax.optimization_barrier((through, states_back))
    inner = inner_grad(head_grad, through_after)
    key_grad = key_grad_local(
        inner, moved, updates, row, uk, cols, state, state_grad, partial, key_mine
    )
    grads = jnp.concatenate([query_grad, key_grad], axis=0)
    extra = jnp.concatenate([squares, squares], axis=0)
    shared = transpose_over(jnp.concatenate([grads, extra], axis=1), "ctx")
    total = jnp.sum(shared, axis=0, keepdims=True)
    final = transpose_over(jnp.broadcast_to(total, (CTX,) + total.shape[1:]), "ctx")
    normalizer = CTX * ROWS * D
    return jnp.sum(final[:HEADS, HD:]) / normalizer, final[:HEADS, :HD], final[HEADS:, :HD]


def solution(mesh):
    placed = (
        P("ctx", "head"),
        P("ctx", None),
        P("ctx", None),
        P("ctx", "head"),
        P("ctx", "head"),
        P("head", None, None),
        P("head", None, None),
        P("head", None),
    )
    return jax.shard_map(
        shards,
        mesh=mesh,
        in_specs=placed,
        out_specs=(P(), P("head", None, None), P("head", None, None)),
        check_vma=False,
    )
```
